32 devices in a mesh: chain: 8 (over z, y), cand: 4 (over x, core).
Axes of the slice: x: 2, y: 2, z: 4, core: 2. Of those that a mesh axis runs over, the one named last changes fastest.
Arguments:
- archive_inputs: float32 [32, 1536], P(None, 'chain'), may hold values from -6 to 6
- candidate_inputs: float32 [32, 512], P(None, 'cand'), may hold values from -6 to 6
- lengthscales: float32 [32], replicated, may hold values from 3 to 10
- factor: float32 [1536, 1536], P('chain'), as said below
Outputs:
- whitened: float32 [1536, 512], P('chain', 'cand')
- corrected_cov: float32 [512, 512], P('chain', 'cand')
The draws below stay inside these ranges and needn't reach their ends.
Inputs may be any that keep to these rules, and one draw needn't show every extreme that they name: factor is lower triangular (zeros above the diagonal); its diagonal lies between 0.2 * sqrt(1536) and 0.5 * sqrt(1536).
All inputs are finite; a program needn't handle non-finite values.
Results may differ from the reference program's by a relative error of at most 0.000076.
Values sent between devices are 32-bit elements; how exact they have to be, the bound alone decides.
A program may use at most 64 MiB of HBM per device.

```python
import math
import jax
import jax.numpy as jnp
from jax import lax

DIMS = 32
ROWS_DEV = 192
CAND_DEV = 128
ARCH = 1536
CANDS = 512


def draw_factor(key, part):
    first_key, second_key = jax.random.split(jax.random.fold_in(key, 7))
    scale_root = jnp.sqrt(jnp.float32(ARCH))
    diagonal = scale_root * jnp.exp(jax.random.uniform(first_key, (ARCH,), jnp.float32, jnp.log(0.2), jnp.log(0.5)))
    spread = jnp.clip(0.12 * jax.random.normal(second_key, (ARCH, ARCH), jnp.float32), -0.6, 0.6)
    lower = jnp.tril(spread, -1) + jnp.diag(diagonal)
    return lower.astype(jnp.float32)


def block_levels(stream_key, extent, shards, least, top_value):
    level = 1.0
    for position, shards_of in shards:
        steps = jax.random.uniform(jax.random.fold_in(jax.random.fold_in(stream_key, 6), position), (shards_of,), jnp.float32, least / len(shards), top_value / len(shards))
        level = level * jnp.repeat(jnp.exp(steps), extent[position] // shards_of).reshape((-1,) + (1,) * (len(extent) - 1 - position))
    return level


def noise(own_key, extent, width, bound, shards=(), dtype=jnp.bfloat16):
    loudness = block_levels(own_key, extent, shards, -0.22, 0.18) if shards else 1.0
    array = jax.random.normal(own_key, extent, jnp.float32) * width * loudness
    return jnp.minimum(jnp.maximum(array, -bound), bound).astype(dtype)


def setup_inputs(seed: int = 0) -> dict:
    splits = jax.random.split(jax.random.key(seed), 5)
    return {
        "archive_inputs": noise(splits[0], (DIMS, ARCH), 1.0, 6.0, ((1, 8),), jnp.float32),
        "candidate_inputs": noise(splits[1], (DIMS, CANDS), 1.0, 6.0, ((1, 4),), jnp.float32),
        "lengthscales": jnp.clip(jnp.exp(jax.random.uniform(splits[2], (DIMS,), jnp.float32, math.log(3.0), math.log(10.0))), 3.0, 10.0),
        "factor": draw_factor(jax.random.fold_in(splits[4], 71), 0),
    }


def matern(first_set, second_set):
    differ = first_set[:, :, None] - second_set[:, None, :]
    radius = jnp.sqrt(5.0 * lax.optimization_barrier(jnp.sum(differ * differ, axis=0)))
    return (1.0 + radius + radius * radius / 3.0) * jnp.exp(-radius)

def reference(archive_inputs, candidate_inputs, lengthscales, factor):
    scaling = 1.0 / lengthscales
    scaled_archive = archive_inputs * scaling[:, None]
    scaled_candidates = candidate_inputs * scaling[:, None]

    def against(row_batch):
        return matern(row_batch, scaled_candidates)
    archive_blocks = scaled_archive.reshape(DIMS, ARCH // ROWS_DEV, ROWS_DEV).transpose(1, 0, 2)
    cross = lax.map(against, archive_blocks).reshape(ARCH, CANDS)
    whitened = jax.scipy.linalg.solve_triangular(factor, cross, lower=True)
    candidate_blocks = scaled_candidates.reshape(DIMS, CANDS // CAND_DEV, CAND_DEV).transpose(1, 0, 2)
    prior_cov = lax.map(against, candidate_blocks).reshape(CANDS, CANDS)
    product = jnp.dot(whitened.T, whitened, precision=lax.Precision.HIGHEST)
    return (whitened, prior_cov - product)
```

```python
import functools
import jax
import jax.numpy as jnp
from jax import lax
from jax.experimental import pallas as pl
from jax.experimental.pallas import tpu as pltpu
from jax.sharding import PartitionSpec as P

MESH = pl.DeviceIdType.MESH
F32 = jnp.float32
BASE = 16


def split(value):
    high = value.astype(jnp.bfloat16)
    return high, (value - high.astype(F32)).astype(jnp.bfloat16)


def product(first, second, transposed=False):
    dims = (((1,), (1 if transposed else 0,)), ((), ()))
    dot = functools.partial(lax.dot_general, dimension_numbers=dims, preferred_element_type=F32)
    return dot(first[0], second[0]) + (dot(first[0], second[1]) + dot(first[1], second[0]))


def matern(rows, columns):
    total = None
    for d in range(columns.shape[0]):
        differ = rows[:, d:d + 1] - columns[d:d + 1, :]
        total = differ * differ if total is None else total + differ * differ
    radius = jnp.sqrt(5.0 * total)
    return (1.0 + radius + radius * radius / 3.0) * jnp.exp(-radius)


def base_inverse(block):
    size = block.shape[0]
    count = size // BASE
    row = lax.broadcasted_iota(jnp.int32, (size, size), 0)
    column = lax.broadcasted_iota(jnp.int32, (size, size), 1)
    same = (row // BASE) == (column // BASE)
    kept = jnp.where(same, block, 0.0)
    packed = functools.reduce(jnp.add, [kept[b * BASE:(b + 1) * BASE] for b in range(count)])
    lane = lax.broadcasted_iota(jnp.int32, (BASE, size), 1) % BASE
    sub = lax.broadcasted_iota(jnp.int32, (BASE, size), 0)
    picked = jnp.concatenate([jnp.where(lane == k, packed, 0.0) for k in range(BASE)], axis=0)
    group = same.astype(F32).astype(jnp.bfloat16)
    spread = None
    rest = picked
    for _ in range(3):
        part = rest.astype(jnp.bfloat16)
        rest = rest - part.astype(F32)
        term = jnp.dot(part, group, preferred_element_type=F32)
        spread = term if spread is None else spread + term
    state = jnp.where(sub == lane, 1.0, 0.0).astype(F32)
    for k in range(BASE):
        coupling = spread[k * BASE:(k + 1) * BASE]
        solved = state[k:k + 1] * (1.0 / coupling[k:k + 1])
        state = jnp.where(sub == k, solved, jnp.where(sub > k, state - coupling * solved, state))
    return jnp.where(same, jnp.concatenate([state] * count, axis=0), 0.0)


def grow_inverse(block, inverse):
    size = block.shape[0]
    row = lax.broadcasted_iota(jnp.int32, (size, size), 0)
    column = lax.broadcasted_iota(jnp.int32, (size, size), 1)
    width = BASE
    while width < size:
        below = ((row // width) == (column // width) + 1) & ((row // (2 * width)) == (column // (2 * width)))
        parts = split(inverse)
        middle = product(parts, split(jnp.where(below, block, 0.0)))
        inverse = inverse - product(split(middle), parts)
        width *= 2
    return inverse


def kernel(sections, cands, archive, candidates, lengths, factor, whitened, covariance,
           both_archive, chosen, points, unit, joined_high, joined_low, panels, peers, columns,
           turned, sums, pieces,
           in_send, in_recv, ch_send, ch_recv, y_send, y_recv, s_send, s_recv,
           pan_send, pan_recv, out_send, out_recv, pass_send, peer_recv, sum_send, sum_recv):
    me = lax.axis_index("chain")
    c = lax.axis_index("cand")
    z, y = me // 2, me % 2
    steps = sections // 2
    core = c % 2
    height = factor.shape[0]
    pair = 2 * height
    width = candidates.shape[1]
    half = width // 2
    ratio = (2 * cands) // sections
    slab = half * ratio
    strip = height // 2
    partner = 2 * z + (1 - y)
    sibling = c + 1 - 2 * core

    def remote(source, target, send, recv, where):
        return pltpu.make_async_remote_copy(
            src_ref=source, dst_ref=target, send_sem=send, recv_sem=recv, device_id=where, device_id_type=MESH)

    barrier = pltpu.get_barrier_semaphore()
    for d in range(1, sections):
        pl.semaphore_signal(barrier, inc=1, device_id=(lax.rem(me + d, sections), c), device_id_type=MESH)
    for d in range(1, cands):
        pl.semaphore_signal(barrier, inc=1, device_id=(me, lax.rem(c + d, cands)), device_id_type=MESH)

    strip_of_pair = factor[:, pl.ds(pl.multiple_of(z * pair, 128), pair)]
    block = jnp.where(y == 0, strip_of_pair[:, :height], strip_of_pair[:, height:])
    small = base_inverse(block)
    scaling = 1.0 / lengths[...]
    both_archive[y] = archive[...]
    owner_cand = (me * slab) // width

    pl.semaphore_wait(barrier, sections + cands - 2)

    send_in = remote(archive, both_archive.at[y], in_send, in_recv, (partner, c))
    send_in.start()

    def chosen_copy(d):
        return remote(candidates, chosen, ch_send.at[d - 1], ch_recv, (me, lax.rem(c + d, cands)))

    @pl.when(c == owner_cand)
    def _():
        for d in range(1, cands):
            chosen_copy(d).start()
        chosen[...] = candidates[...]

    inverse = grow_inverse(block, small)
    inverse_parts = split(inverse)
    zeros = jnp.zeros((height, height), F32)
    lane = lax.broadcasted_iota(jnp.int32, (height, pair), 1)
    near = product(inverse_parts, split(strip_of_pair))
    unit[0, y] = jnp.where(
        y == 0, jnp.concatenate([inverse, zeros], axis=1),
        jnp.where(lane < height, near, jnp.concatenate([zeros, inverse], axis=1)))

    mine = pl.ds(pl.multiple_of(core * strip, 8), strip)
    others = pl.ds(pl.multiple_of((1 - core) * strip, 8), strip)

    def across(e):
        area = unit.at[e, y, mine]
        return remote(area, area, y_send.at[e], y_recv.at[e], (partner, c))

    def across_recv(e):
        area = unit.at[e, 1 - y, mine]
        return remote(area, area, y_send.at[e], y_recv.at[e], (partner, c))

    def beside(e):
        area = unit.at[e, 1 - y, mine]
        return remote(area, area, s_send.at[e], s_recv.at[e], (me, sibling))

    def beside_recv(e):
        area = unit.at[e, 1 - y, others]
        return remote(area, area, s_send.at[e], s_recv.at[e], (me, sibling))

    across(0).start()
    for j in range(steps - 1):
        @pl.when(z > j)
        def _(j=j):
            unit[j + 1, y] = product(inverse_parts, split(factor[:, j * pair:(j + 1) * pair]))
            across(j + 1).start()

    points[...] = jnp.transpose(candidates[...] * scaling)
    own_points = points[pl.ds(pl.multiple_of(y * half, 8), half), :]
    send_in.wait_send()
    remote(archive, both_archive.at[1 - y], in_send, in_recv, (partner, c)).wait_recv()
    both = jnp.concatenate([both_archive[0], both_archive[1]], axis=1) * scaling
    cross = matern(own_points, both)

    across_recv(0).wait_recv()
    beside(0).start()
    for j in range(steps - 1):
        @pl.when(z > j)
        def _(j=j):
            across_recv(j + 1).wait_recv()
            beside(j + 1).start()
    beside_recv(0).wait_recv()
    upper = unit[0, 0]
    lower = unit[0, 1]
    full = jnp.concatenate(
        [jnp.where(lane < height, upper, 0.0), jnp.where(lane < height, 0.0, lower)], axis=0)
    columns[y] = product(split(cross), split(full), transposed=True)
    high, low = split(jnp.concatenate(
        [jnp.zeros((height, pair), F32), jnp.where(lane < height, lower, 0.0)], axis=0))
    joined_high[0] = high
    joined_low[0] = low

    def onward(j):
        return remote(panels.at[j], panels.at[j], pan_send.at[j], pan_recv.at[j],
                      (lax.rem(me + 2, sections), c))

    for j in range(steps - 1):
        @pl.when(z > j)
        def _(j=j):
            beside_recv(j + 1).wait_recv()
            high, low = split(unit[j + 1].reshape(pair, pair))
            joined_high[j + 1] = high
            joined_low[j + 1] = low
            onward(j).wait_recv()
            if j < steps - 2:
                @pl.when(z < steps - 1)
                def _():
                    onward(j).start()
            columns[y] = columns[y] - product(
                split(panels[j]), (joined_high[j + 1], joined_low[j + 1]), transposed=True)

    reduced = columns[y]
    solved = reduced - product(split(reduced), (joined_high[0], joined_low[0]), transposed=True)
    columns[y] = solved

    def launch(j):
        return remote(columns.at[y], panels.at[j], out_send.at[0], pan_recv.at[j], (lax.rem(me + 2, sections), c))

    for j in range(steps - 1):
        @pl.when(z == j)
        def _(j=j):
            launch(j).start()

    def to_peer(d):
        return remote(columns.at[y], peers.at[c], out_send.at[1 + d], peer_recv.at[c], (me, lax.rem(c + 2 * d, cands)))

    def from_peer(q):
        return remote(columns.at[y], peers.at[q], out_send.at[1], peer_recv.at[q], (me, sibling))

    def pass_on(d):
        q = lax.rem(c + 2 * d, cands)
        return remote(peers.at[q], peers.at[q], pass_send.at[d], peer_recv.at[q], (me, sibling))

    half_count = cands // 2
    for d in range(1, half_count):
        to_peer(d).start()
    to_sibling = remote(columns.at[y], peers.at[c], out_send.at[1], peer_recv.at[c], (me, sibling))
    to_sibling.start()
    to_partner = remote(columns.at[y], columns.at[y], out_send.at[1 + half_count], out_recv, (partner, c))
    to_partner.start()
    peers[c] = solved

    @pl.when(c != owner_cand)
    def _():
        remote(candidates, chosen, ch_send.at[0], ch_recv, (me, sibling)).wait_recv()

    points[...] = jnp.transpose(chosen[...] * scaling)
    within = pl.multiple_of((me * slab) % width, 8)
    prior = matern(points[pl.ds(within, slab), :], candidates[...] * scaling)
    covariance[...] = prior

    for d in range(1, half_count):
        q = lax.rem(c + 2 * d, cands)
        from_peer(q).wait_recv()
        pass_on(d).start()
    remote(columns.at[y], columns.at[1 - y], out_send.at[1], out_recv, (partner, c)).wait_recv()
    own_columns = columns[...].reshape(width, pair)
    for d in range(half_count):
        from_peer(lax.rem(sibling + 2 * d, cands)).wait_recv()

    gram = product(split(peers[...].reshape(cands * half, pair)), split(own_columns), transposed=True)
    pieces[...] = gram.reshape(cands, half, width)

    def piece_copy(q):
        group = 2 * q + y
        return remote(pieces.at[q], sums.at[z, group % ratio], sum_send.at[q],
                      sum_recv.at[z, group % ratio], (group // ratio, c))

    for q in range(cands):
        group = 2 * q + y

        @pl.when(group // ratio != me)
        def _(q=q):
            piece_copy(q).start()

        @pl.when(group // ratio == me)
        def _(q=q, group=group):
            sums[z, group % ratio] = pieces[q]

    turned[...] = jnp.transpose(own_columns)
    whitened[...] = turned[pl.ds(pl.multiple_of(y * height, 8), height), :]

    for k in range(ratio):
        for step in range(steps):
            sender = 2 * step + lax.rem(ratio * me + k, 2)

            @pl.when(sender != me)
            def _(k=k, step=step):
                remote(pieces.at[0], sums.at[step, k], sum_send.at[0], sum_recv.at[step, k], (partner, c)).wait_recv()
        total = functools.reduce(jnp.add, [sums[step, k] for step in range(steps)])
        covariance[k * half:(k + 1) * half] = covariance[k * half:(k + 1) * half] - total

    @pl.when(c == owner_cand)
    def _():
        for d in range(1, cands):
            chosen_copy(d).wait_send()
    across(0).wait_send()
    beside(0).wait_send()
    for j in range(steps - 1):
        @pl.when(z > j)
        def _(j=j):
            across(j + 1).wait_send()
            beside(j + 1).wait_send()
            if j < steps - 2:
                @pl.when(z < steps - 1)
                def _():
                    onward(j).wait_send()

        @pl.when(z == j)
        def _(j=j):
            launch(j).wait_send()
    for d in range(1, half_count):
        to_peer(d).wait_send()
        pass_on(d).wait_send()
    to_sibling.wait_send()
    to_partner.wait_send()
    for q in range(cands):
        @pl.when((2 * q + y) // ratio != me)
        def _(q=q):
            piece_copy(q).wait_send()


def shards(sections, cands, archive, candidates, lengths, factor):
    dims, height = archive.shape
    width = candidates.shape[1]
    pair, half, steps = 2 * height, width // 2, sections // 2
    ratio = (2 * cands) // sections
    vmem = pl.BlockSpec(memory_space=pltpu.VMEM)
    dma = pltpu.SemaphoreType.DMA
    return pl.pallas_call(
        functools.partial(kernel, sections, cands),
        out_shape=(jax.ShapeDtypeStruct((height, width), F32), jax.ShapeDtypeStruct((half * ratio, width), F32)),
        in_specs=[vmem] * 4,
        out_specs=(vmem, vmem),
        scratch_shapes=[
            pltpu.VMEM((2, dims, height), F32),
            pltpu.VMEM((dims, width), F32),
            pltpu.VMEM((width, dims), F32),
            pltpu.VMEM((steps, 2, height, pair), F32),
            pltpu.VMEM((steps, pair, pair), jnp.bfloat16),
            pltpu.VMEM((steps, pair, pair), jnp.bfloat16),
            pltpu.VMEM((steps - 1, half, pair), F32),
            pltpu.VMEM((cands, half, pair), F32),
            pltpu.VMEM((2, half, pair), F32),
            pltpu.VMEM((pair, width), F32),
            pltpu.VMEM((steps, ratio, half, width), F32),
            pltpu.VMEM((cands, half, width), F32),
            dma, dma,
            dma((cands - 1,)), dma,
            dma((steps,)), dma((steps,)), dma((steps,)), dma((steps,)),
            dma((steps - 1,)), dma((steps - 1,)),
            dma((2 + cands // 2,)), dma,
            dma((cands // 2,)), dma((cands,)),
            dma((cands,)), dma((steps, ratio)),
        ],
        compiler_params=pltpu.CompilerParams(
            collective_id=0, has_side_effects=True, vmem_limit_bytes=40 * 1024 * 1024),
    )(archive, candidates, lengths.reshape(dims, 1), factor)


def solution(mesh):
    return jax.shard_map(
        functools.partial(shards, mesh.shape["chain"], mesh.shape["cand"]),
        mesh=mesh,
        in_specs=(P(None, "chain"), P(None, "cand"), P(), P("chain", None)),
        out_specs=(P("chain", "cand"), P("chain", "cand")),
        check_vma=False,
    )
```

```python
import functools
import jax
import jax.numpy as jnp
from jax import lax
from jax.experimental import pallas as pl
from jax.experimental.pallas import tpu as pltpu
from jax.sharding import PartitionSpec as P

MESH = pl.DeviceIdType.MESH
F32 = jnp.float32
BASE = 16


def split(value):
    high = value.astype(jnp.bfloat16)
    return high, (value - high.astype(F32)).astype(jnp.bfloat16)


def product(first, second, transposed=False):
    dims = (((1,), (1 if transposed else 0,)), ((), ()))
    dot = functools.partial(lax.dot_general, dimension_numbers=dims, preferred_element_type=F32)
    return dot(first[0], second[0]) + (dot(first[0], second[1]) + dot(first[1], second[0]))


def matern(rows, columns):
    total = None
    for d in range(columns.shape[0]):
        differ = rows[:, d:d + 1] - columns[d:d + 1, :]
        total = differ * differ if total is None else total + differ * differ
    radius = jnp.sqrt(5.0 * total)
    return (1.0 + radius + radius * radius / 3.0) * jnp.exp(-radius)


def base_inverse(block):
    size = block.shape[0]
    count = size // BASE
    row = lax.broadcasted_iota(jnp.int32, (size, size), 0)
    column = lax.broadcasted_iota(jnp.int32, (size, size), 1)
    same = (row // BASE) == (column // BASE)
    kept = jnp.where(same, block, 0.0)
    packed = functools.reduce(jnp.add, [kept[b * BASE:(b + 1) * BASE] for b in range(count)])
    lane = lax.broadcasted_iota(jnp.int32, (BASE, size), 1) % BASE
    sub = lax.broadcasted_iota(jnp.int32, (BASE, size), 0)
    picked = jnp.concatenate([jnp.where(lane == k, packed, 0.0) for k in range(BASE)], axis=0)
    group = same.astype(F32).astype(jnp.bfloat16)
    spread = None
    rest = picked
    for _ in range(3):
        part = rest.astype(jnp.bfloat16)
        rest = rest - part.astype(F32)
        term = jnp.dot(part, group, preferred_element_type=F32)
        spread = term if spread is None else spread + term
    state = jnp.where(sub == lane, 1.0, 0.0).astype(F32)
    for k in range(BASE):
        coupling = spread[k * BASE:(k + 1) * BASE]
        solved = state[k:k + 1] * (1.0 / coupling[k:k + 1])
        state = jnp.where(sub == k, solved, jnp.where(sub > k, state - coupling * solved, state))
    return jnp.where(same, jnp.concatenate([state] * count, axis=0), 0.0)


def grow_inverse(block, inverse):
    size = block.shape[0]
    row = lax.broadcasted_iota(jnp.int32, (size, size), 0)
    column = lax.broadcasted_iota(jnp.int32, (size, size), 1)
    width = BASE
    while width < size:
        above = ((row // width) + 1 == (column // width)) & ((row // (2 * width)) == (column // (2 * width)))
        parts = split(inverse)
        middle = product(parts, split(jnp.where(above, block, 0.0)))
        inverse = inverse - product(split(middle), parts)
        width *= 2
    return inverse


def kernel(sections, cands, archive, candidates, lengths, factor, whitened, covariance,
           both_archive, near, far, own_candidates, own_lengths, chosen, points, inverses,
           high_weights, low_weights, panels, peers, columns, turned, sums, pieces,
           load, far_load, in_send, in_recv, ch_send, ch_recv, y_send, y_recv, s_send, s_recv,
           pan_send, pan_recv, out_send, out_recv, pass_send, peer_recv, sum_send, sum_recv):
    me = lax.axis_index("chain")
    c = lax.axis_index("cand")
    z, y = me // 2, me % 2
    steps = sections // 2
    core = c % 2
    height = factor.shape[0]
    pair = 2 * height
    cover = -(-height // 128) * 128
    width = candidates.shape[1]
    half = width // 2
    ratio = (2 * cands) // sections
    slab = half * ratio
    strip = height // 2
    partner = 2 * z + (1 - y)
    sibling = c + 1 - 2 * core
    mine = pl.ds(pl.multiple_of(core * strip, 8), strip)
    others = pl.ds(pl.multiple_of((1 - core) * strip, 8), strip)
    diagonal = pl.multiple_of(z * pair, 128)

    def remote(source, target, send, recv, where):
        return pltpu.make_async_remote_copy(
            src_ref=source, dst_ref=target, send_sem=send, recv_sem=recv, device_id=where, device_id_type=MESH)

    def far_copy(j):
        return pltpu.make_async_copy(factor.at[:, j * pair:(j + 1) * pair], far.at[j, y], far_load.at[j])

    near_copy = pltpu.make_async_copy(factor.at[:, pl.ds(diagonal, pair)], near.at[y], load.at[0])
    lengths_copy = pltpu.make_async_copy(lengths, own_lengths, load.at[1])
    candidates_copy = pltpu.make_async_copy(candidates, own_candidates, load.at[2])
    archive_copy = pltpu.make_async_copy(archive, both_archive.at[y], load.at[3])
    near_copy.start()
    lengths_copy.start()
    candidates_copy.start()
    archive_copy.start()

    barrier = pltpu.get_barrier_semaphore()
    for d in range(1, sections):
        pl.semaphore_signal(barrier, inc=1, device_id=(lax.rem(me + d, sections), c), device_id_type=MESH)
    for d in range(1, cands):
        pl.semaphore_signal(barrier, inc=1, device_id=(me, lax.rem(c + d, cands)), device_id_type=MESH)
    for j in range(steps - 1):
        @pl.when(z > j)
        def _(j=j):
            far_copy(j).start()

    near_copy.wait()
    strip_of_pair = near[y]
    block = jnp.where(y == 0, strip_of_pair[:, :height], strip_of_pair[:, height:])
    small = jnp.transpose(base_inverse(block))
    block = jnp.transpose(block)
    lengths_copy.wait()
    candidates_copy.wait()
    archive_copy.wait()
    scale_row = 1.0 / own_lengths[...]
    scaling = jnp.transpose(jnp.broadcast_to(scale_row, (8, scale_row.shape[1])))[:, :1]
    owner_cand = (me * slab) // width

    pl.semaphore_wait(barrier, sections + cands - 2)

    send_in = remote(archive, both_archive.at[y], in_send, in_recv, (partner, c))
    send_in.start()

    def area(e, who, rows):
        if e == 0:
            return inverses.at[who, rows]
        if e == 1:
            return near.at[1, rows, pl.ds(0, cover)]
        return far.at[e - 2, who, rows]

    def across(e):
        if e == 0:
            source = inverses.at[y, mine]
        elif e == 1:
            source = factor.at[mine, pl.ds(diagonal, cover)]
        else:
            source = factor.at[mine, pl.ds((e - 2) * pair, pair)]
        return remote(source, area(e, y, mine), y_send.at[e], y_recv.at[e], (partner, c))

    def across_recv(e):
        return remote(area(e, 1 - y, mine), area(e, 1 - y, mine), y_send.at[e], y_recv.at[e], (partner, c))

    def beside(e):
        return remote(area(e, 1 - y, mine), area(e, 1 - y, mine), s_send.at[e], s_recv.at[e], (me, sibling))

    def beside_recv(e):
        return remote(area(e, 1 - y, others), area(e, 1 - y, others), s_send.at[e], s_recv.at[e], (me, sibling))

    @pl.when(y == 1)
    def _():
        across(1).start()
    for j in range(steps - 1):
        @pl.when(z > j)
        def _(j=j):
            across(j + 2).start()

    def chosen_copy(d):
        return remote(candidates, chosen, ch_send.at[d - 1], ch_recv, (me, lax.rem(c + d, cands)))

    @pl.when(c == owner_cand)
    def _():
        for d in range(1, cands):
            chosen_copy(d).start()
        chosen[...] = own_candidates[...]

    inverses[y] = grow_inverse(block, small)
    across(0).start()

    @pl.when(y == 0)
    def _():
        across_recv(1).wait_recv()
        beside(1).start()

    points[...] = jnp.transpose(own_candidates[...] * scaling)
    own_points = points[pl.ds(pl.multiple_of(y * half, 8), half), :]
    send_in.wait_send()
    remote(archive, both_archive.at[1 - y], in_send, in_recv, (partner, c)).wait_recv()
    upper_cross = split(matern(own_points, both_archive[0] * scaling))
    lower_cross = split(matern(own_points, both_archive[1] * scaling))

    @pl.when(y == 0)
    def _():
        beside_recv(1).wait_recv()

    coupling = split(jnp.transpose(near[1][:, :height]))
    across_recv(0).wait_recv()
    beside(0).start()
    for j in range(steps - 1):
        @pl.when(z > j)
        def _(j=j):
            far_copy(j).wait()
            across_recv(j + 2).wait_recv()
            beside(j + 2).start()
    beside_recv(0).wait_recv()
    upper = split(inverses[0])
    lower = split(inverses[1])
    between = split(product(coupling, lower))
    first = product(upper_cross, upper)
    second = product(lower_cross, lower) - product(split(first), between)
    columns[y] = jnp.concatenate([first, second], axis=1)

    @pl.when(z > 0)
    def _():
        corner = -product(upper, between)
        whole = split(jnp.concatenate([
            jnp.concatenate([inverses[0], corner], axis=1),
            jnp.concatenate([jnp.zeros((height, height), F32), inverses[1]], axis=1)], axis=0))
        for j in range(steps - 1):
            @pl.when(z > j)
            def _(j=j):
                beside_recv(j + 2).wait_recv()
                weights = product(split(jnp.transpose(far[j].reshape(pair, pair))), whole)
                high, low = split(weights)
                high_weights[j] = high
                low_weights[j] = low

    def onward(j):
        return remote(panels.at[j], panels.at[j], pan_send.at[j], pan_recv.at[j],
                      (lax.rem(me + 2, sections), c))

    for j in range(steps - 1):
        @pl.when(z > j)
        def _(j=j):
            onward(j).wait_recv()
            if j < steps - 2:
                @pl.when(z < steps - 1)
                def _():
                    onward(j).start()
            columns[y] = columns[y] - product(split(panels[j]), (high_weights[j], low_weights[j]))

    def launch(j):
        return remote(columns.at[y], panels.at[j], out_send.at[0], pan_recv.at[j], (lax.rem(me + 2, sections), c))

    for j in range(steps - 1):
        @pl.when(z == j)
        def _(j=j):
            launch(j).start()

    def to_peer(d):
        return remote(columns.at[y], peers.at[c], out_send.at[1 + d], peer_recv.at[c], (me, lax.rem(c + 2 * d, cands)))

    def from_peer(q):
        return remote(columns.at[y], peers.at[q], out_send.at[1], peer_recv.at[q], (me, sibling))

    def pass_on(d):
        q = lax.rem(c + 2 * d, cands)
        return remote(peers.at[q], peers.at[q], pass_send.at[d], peer_recv.at[q], (me, sibling))

    half_count = cands // 2
    for d in range(1, half_count):
        to_peer(d).start()
    to_partner = remote(columns.at[y], columns.at[y], out_send.at[1 + half_count], out_recv, (partner, c))
    to_partner.start()
    to_sibling = remote(columns.at[y], peers.at[c], out_send.at[1], peer_recv.at[c], (me, sibling))
    to_sibling.start()
    peers[c] = columns[y]

    @pl.when(c != owner_cand)
    def _():
        remote(candidates, chosen, ch_send.at[0], ch_recv, (me, sibling)).wait_recv()

    points[...] = jnp.transpose(chosen[...] * scaling)
    within = pl.multiple_of((me * slab) % width, 8)
    covariance[...] = matern(points[pl.ds(within, slab), :], own_candidates[...] * scaling)

    remote(columns.at[y], columns.at[1 - y], out_send.at[1], out_recv, (partner, c)).wait_recv()
    turned[...] = jnp.transpose(columns[...].reshape(width, pair))
    facing = split(turned[...])

    def piece_copy(q):
        group = 2 * q + y
        return remote(pieces.at[q], sums.at[z, group % ratio], sum_send.at[q],
                      sum_recv.at[z, group % ratio], (group // ratio, c))

    def piece(q):
        group = 2 * q + y
        pieces[q] = product(split(peers[q]), facing)

        @pl.when(group // ratio != me)
        def _():
            piece_copy(q).start()

        @pl.when(group // ratio == me)
        def _():
            sums[z, group % ratio] = pieces[q]

    piece(c)
    from_peer(sibling).wait_recv()
    piece(sibling)
    for d in range(1, half_count):
        q = lax.rem(c + 2 * d, cands)
        from_peer(q).wait_recv()
        pass_on(d).start()
        piece(q)
    for d in range(1, half_count):
        q = lax.rem(sibling + 2 * d, cands)
        from_peer(q).wait_recv()
        piece(q)

    whitened[...] = turned[pl.ds(pl.multiple_of(y * height, 8), height), :]

    for k in range(ratio):
        for step in range(steps):
            sender = 2 * step + lax.rem(ratio * me + k, 2)

            @pl.when(sender != me)
            def _(k=k, step=step):
                remote(pieces.at[0], sums.at[step, k], sum_send.at[0], sum_recv.at[step, k], (partner, c)).wait_recv()
        total = functools.reduce(jnp.add, [sums[step, k] for step in range(steps)])
        covariance[k * half:(k + 1) * half] = covariance[k * half:(k + 1) * half] - total

    @pl.when(c == owner_cand)
    def _():
        for d in range(1, cands):
            chosen_copy(d).wait_send()
    across(0).wait_send()
    beside(0).wait_send()

    @pl.when(y == 1)
    def _():
        across(1).wait_send()

    @pl.when(y == 0)
    def _():
        beside(1).wait_send()
    for j in range(steps - 1):
        @pl.when(z > j)
        def _(j=j):
            across(j + 2).wait_send()
            beside(j + 2).wait_send()
            if j < steps - 2:
                @pl.when(z < steps - 1)
                def _():
                    onward(j).wait_send()

        @pl.when(z == j)
        def _(j=j):
            launch(j).wait_send()
    for d in range(1, half_count):
        to_peer(d).wait_send()
        pass_on(d).wait_send()
    to_sibling.wait_send()
    to_partner.wait_send()
    for q in range(cands):
        @pl.when((2 * q + y) // ratio != me)
        def _(q=q):
            piece_copy(q).wait_send()


def shards(sections, cands, archive, candidates, lengths, factor):
    dims, height = archive.shape
    width = candidates.shape[1]
    pair, half, steps = 2 * height, width // 2, sections // 2
    ratio = (2 * cands) // sections
    vmem = pl.BlockSpec(memory_space=pltpu.VMEM)
    hbm = pl.BlockSpec(memory_space=pltpu.HBM)
    dma = pltpu.SemaphoreType.DMA
    return pl.pallas_call(
        functools.partial(kernel, sections, cands),
        out_shape=(jax.ShapeDtypeStruct((height, width), F32), jax.ShapeDtypeStruct((half * ratio, width), F32)),
        in_specs=[hbm] * 4,
        out_specs=(vmem, vmem),
        scratch_shapes=[
            pltpu.VMEM((2, dims, height), F32),
            pltpu.VMEM((2, height, pair), F32),
            pltpu.VMEM((steps - 1, 2, height, pair), F32),
            pltpu.VMEM((dims, width), F32),
            pltpu.VMEM((1, dims), F32),
            pltpu.VMEM((dims, width), F32),
            pltpu.VMEM((width, dims), F32),
            pltpu.VMEM((2, height, height), F32),
            pltpu.VMEM((steps - 1, pair, pair), jnp.bfloat16),
            pltpu.VMEM((steps - 1, pair, pair), jnp.bfloat16),
            pltpu.VMEM((steps - 1, half, pair), F32),
            pltpu.VMEM((cands, half, pair), F32),
            pltpu.VMEM((2, half, pair), F32),
            pltpu.VMEM((pair, width), F32),
            pltpu.VMEM((steps, ratio, half, width), F32),
            pltpu.VMEM((cands, half, width), F32),
            dma((4,)), dma((steps - 1,)),
            dma, dma,
            dma((cands - 1,)), dma,
            dma((steps + 1,)), dma((steps + 1,)), dma((steps + 1,)), dma((steps + 1,)),
            dma((steps - 1,)), dma((steps - 1,)),
            dma((2 + cands // 2,)), dma,
            dma((cands // 2,)), dma((cands,)),
            dma((cands,)), dma((steps, ratio)),
        ],
        compiler_params=pltpu.CompilerParams(
            collective_id=0, has_side_effects=True, vmem_limit_bytes=62 * 1024 * 1024),
    )(archive, candidates, lengths.reshape(1, dims), factor)


def solution(mesh):
    return jax.shard_map(
        functools.partial(shards, mesh.shape["chain"], mesh.shape["cand"]),
        mesh=mesh,
        in_specs=(P(None, "chain"), P(None, "cand"), P(), P("chain", None)),
        out_specs=(P("chain", "cand"), P("chain", "cand")),
        check_vma=False,
    )
```

```python
import functools
import jax
import jax.numpy as jnp
from jax import lax
from jax.experimental import pallas as pl
from jax.experimental.pallas import tpu as pltpu
from jax.sharding import PartitionSpec as P

MESH = pl.DeviceIdType.MESH
F32 = jnp.float32
BASE = 32


def split(value):
    high = value.astype(jnp.bfloat16)
    return high, (value - high.astype(F32)).astype(jnp.bfloat16)


def product(first, second, transposed=False):
    dims = (((1,), (1 if transposed else 0,)), ((), ()))
    dot = functools.partial(lax.dot_general, dimension_numbers=dims, preferred_element_type=F32)
    return dot(first[0], second[0]) + (dot(first[0], second[1]) + dot(first[1], second[0]))


def matern(rows, columns):
    total = None
    for d in range(columns.shape[0]):
        differ = rows[:, d:d + 1] - columns[d:d + 1, :]
        total = differ * differ if total is None else total + differ * differ
    radius = jnp.sqrt(5.0 * total)
    return (1.0 + radius + radius * radius / 3.0) * jnp.exp(-radius)


def base_inverse(block):
    size = block.shape[0]
    count = size // BASE
    row = lax.broadcasted_iota(jnp.int32, (size, size), 0)
    column = lax.broadcasted_iota(jnp.int32, (size, size), 1)
    same = (row // BASE) == (column // BASE)
    kept = jnp.where(same, block, 0.0)
    packed = functools.reduce(jnp.add, [kept[b * BASE:(b + 1) * BASE] for b in range(count)])
    lane = lax.broadcasted_iota(jnp.int32, (BASE, size), 1) % BASE
    sub = lax.broadcasted_iota(jnp.int32, (BASE, size), 0)
    picked = jnp.concatenate([jnp.where(lane == k, packed, 0.0) for k in range(BASE)], axis=0)
    group = same.astype(F32).astype(jnp.bfloat16)
    spread = None
    rest = picked
    for _ in range(3):
        part = rest.astype(jnp.bfloat16)
        rest = rest - part.astype(F32)
        term = jnp.dot(part, group, preferred_element_type=F32)
        spread = term if spread is None else spread + term
    state = jnp.where(sub == lane, 1.0, 0.0).astype(F32)
    for k in range(BASE):
        coupling = spread[k * BASE:(k + 1) * BASE]
        solved = state[k:k + 1] * (1.0 / coupling[k:k + 1])
        state = jnp.where(sub == k, solved, jnp.where(sub > k, state - coupling * solved, state))
    return jnp.where(same, jnp.concatenate([state] * count, axis=0), 0.0)


def grow_inverse(block, inverse, start, end):
    size = block.shape[0]
    row = lax.broadcasted_iota(jnp.int32, (size, size), 0)
    column = lax.broadcasted_iota(jnp.int32, (size, size), 1)
    width = start
    while width < end:
        above = ((row // width) + 1 == (column // width)) & ((row // (2 * width)) == (column // (2 * width)))
        parts = split(inverse)
        middle = product(parts, split(jnp.where(above, block, 0.0)))
        inverse = inverse - product(split(middle), parts)
        width *= 2
    return inverse


def kernel(sections, cands, archive, candidates, lengths, factor, whitened, covariance,
           both_archive, near, far, own_candidates, own_lengths, chosen, points, inverses,
           high_weights, low_weights, panels, peers, columns, turned, sums, pieces,
           load, far_load, in_send, in_recv, ch_send, ch_recv, y_send, y_recv, s_send, s_recv,
           pan_send, pan_recv, out_send, out_recv, pass_send, peer_recv, sum_send, sum_recv):
    me = lax.axis_index("chain")
    c = lax.axis_index("cand")
    z, y = me // 2, me % 2
    steps = sections // 2
    core = c % 2
    height = factor.shape[0]
    pair = 2 * height
    cover = -(-height // 128) * 128
    width = candidates.shape[1]
    half = width // 2
    ratio = (2 * cands) // sections
    slab = half * ratio
    strip = height // 2
    partner = 2 * z + (1 - y)
    sibling = c + 1 - 2 * core
    mine = pl.ds(pl.multiple_of(core * strip, 8), strip)
    others = pl.ds(pl.multiple_of((1 - core) * strip, 8), strip)
    diagonal = pl.multiple_of(z * pair, 128)

    def remote(source, target, send, recv, where):
        return pltpu.make_async_remote_copy(
            src_ref=source, dst_ref=target, send_sem=send, recv_sem=recv, device_id=where, device_id_type=MESH)

    def far_copy(j):
        return pltpu.make_async_copy(factor.at[:, j * pair:(j + 1) * pair], far.at[j, y], far_load.at[j])

    near_copy = pltpu.make_async_copy(factor.at[:, pl.ds(diagonal, pair)], near.at[y], load.at[0])
    lengths_copy = pltpu.make_async_copy(lengths, own_lengths, load.at[1])
    candidates_copy = pltpu.make_async_copy(candidates, own_candidates, load.at[2])
    archive_copy = pltpu.make_async_copy(archive, both_archive.at[y], load.at[3])
    near_copy.start()
    lengths_copy.start()
    candidates_copy.start()
    archive_copy.start()

    barrier = pltpu.get_barrier_semaphore()
    for d in range(1, sections):
        pl.semaphore_signal(barrier, inc=1, device_id=(lax.rem(me + d, sections), c), device_id_type=MESH)
    for d in range(1, cands):
        pl.semaphore_signal(barrier, inc=1, device_id=(me, lax.rem(c + d, cands)), device_id_type=MESH)
    for j in range(steps - 1):
        @pl.when(z > j)
        def _(j=j):
            far_copy(j).start()

    near_copy.wait()
    strip_of_pair = near[y]
    block = jnp.where(y == 0, strip_of_pair[:, :height], strip_of_pair[:, height:])
    small = jnp.transpose(base_inverse(block))
    block = jnp.transpose(block)
    small = grow_inverse(block, small, BASE, 2 * BASE)
    lengths_copy.wait()
    candidates_copy.wait()
    archive_copy.wait()
    scale_row = 1.0 / own_lengths[...]
    scaling = jnp.transpose(jnp.broadcast_to(scale_row, (8, scale_row.shape[1])))[:, :1]
    owner_cand = (me * slab) // width

    pl.semaphore_wait(barrier, sections + cands - 2)

    send_in = remote(archive, both_archive.at[y], in_send, in_recv, (partner, c))
    send_in.start()

    def area(e, who, rows):
        if e == 0:
            return inverses.at[who, rows]
        if e == 1:
            return near.at[1, rows, pl.ds(0, cover)]
        return far.at[e - 2, who, rows]

    def across(e):
        if e == 0:
            source = inverses.at[y, mine]
        elif e == 1:
            source = factor.at[mine, pl.ds(diagonal, cover)]
        else:
            source = factor.at[mine, pl.ds((e - 2) * pair, pair)]
        return remote(source, area(e, y, mine), y_send.at[e], y_recv.at[e], (partner, c))

    def across_recv(e):
        return remote(area(e, 1 - y, mine), area(e, 1 - y, mine), y_send.at[e], y_recv.at[e], (partner, c))

    def beside(e):
        return remote(area(e, 1 - y, mine), area(e, 1 - y, mine), s_send.at[e], s_recv.at[e], (me, sibling))

    def beside_recv(e):
        return remote(area(e, 1 - y, others), area(e, 1 - y, others), s_send.at[e], s_recv.at[e], (me, sibling))

    @pl.when(y == 1)
    def _():
        across(1).start()
    early = min(2, steps - 1)
    for j in range(early):
        @pl.when(z > j)
        def _(j=j):
            across(j + 2).start()

    def chosen_copy(d):
        return remote(candidates, chosen, ch_send.at[d - 1], ch_recv, (me, lax.rem(c + d, cands)))

    @pl.when(c == owner_cand)
    def _():
        for d in range(1, cands):
            chosen_copy(d).start()
        chosen[...] = own_candidates[...]

    inverses[y] = grow_inverse(block, small, 2 * BASE, height)
    across(0).start()
    for j in range(early, steps - 1):
        @pl.when(z > j)
        def _(j=j):
            across(j + 2).start()

    @pl.when(y == 0)
    def _():
        across_recv(1).wait_recv()
        beside(1).start()

    points[...] = jnp.transpose(own_candidates[...] * scaling)
    own_points = points[pl.ds(pl.multiple_of(y * half, 8), half), :]
    send_in.wait_send()
    remote(archive, both_archive.at[1 - y], in_send, in_recv, (partner, c)).wait_recv()
    upper_cross = split(matern(own_points, both_archive[0] * scaling))
    lower_cross = split(matern(own_points, both_archive[1] * scaling))

    @pl.when(y == 0)
    def _():
        beside_recv(1).wait_recv()

    coupling = split(jnp.transpose(near[1][:, :height]))

    def pass_far(j):
        far_copy(j).wait()
        across_recv(j + 2).wait_recv()
        beside(j + 2).start()

    def turn_far(j):
        beside_recv(j + 2).wait_recv()
        high, low = split(jnp.transpose(far[j].reshape(pair, pair)))
        high_weights[j] = high
        low_weights[j] = low

    for j in range(early):
        @pl.when(z > j)
        def _(j=j):
            pass_far(j)
    across_recv(0).wait_recv()
    beside(0).start()
    for j in range(early):
        @pl.when(z > j)
        def _(j=j):
            turn_far(j)
    beside_recv(0).wait_recv()
    upper = split(inverses[0])
    lower = split(inverses[1])
    between = split(product(coupling, lower))
    first = product(upper_cross, upper)
    second = product(lower_cross, lower) - product(split(first), between)
    columns[y] = jnp.concatenate([first, second], axis=1)

    @pl.when(z > 0)
    def _():
        corner = -product(upper, between)
        whole = split(jnp.concatenate([
            jnp.concatenate([inverses[0], corner], axis=1),
            jnp.concatenate([jnp.zeros((height, height), F32), inverses[1]], axis=1)], axis=0))
        for j in range(steps - 1):
            @pl.when(z > j)
            def _(j=j):
                if j >= early:
                    pass_far(j)
                    turn_far(j)
                weights = product((high_weights[j], low_weights[j]), whole)
                high, low = split(weights)
                high_weights[j] = high
                low_weights[j] = low

    def onward(j):
        return remote(panels.at[j], panels.at[j], pan_send.at[j], pan_recv.at[j],
                      (lax.rem(me + 2, sections), c))

    for j in range(steps - 1):
        @pl.when(z > j)
        def _(j=j):
            onward(j).wait_recv()
            if j < steps - 2:
                @pl.when(z < steps - 1)
                def _():
                    onward(j).start()
            columns[y] = columns[y] - product(split(panels[j]), (high_weights[j], low_weights[j]))

    def launch(j):
        return remote(columns.at[y], panels.at[j], out_send.at[0], pan_recv.at[j], (lax.rem(me + 2, sections), c))

    for j in range(steps - 1):
        @pl.when(z == j)
        def _(j=j):
            launch(j).start()

    def to_peer(d):
        return remote(columns.at[y], peers.at[c], out_send.at[1 + d], peer_recv.at[c], (me, lax.rem(c + 2 * d, cands)))

    def from_peer(q):
        return remote(columns.at[y], peers.at[q], out_send.at[1], peer_recv.at[q], (me, sibling))

    def pass_on(d):
        q = lax.rem(c + 2 * d, cands)
        return remote(peers.at[q], peers.at[q], pass_send.at[d], peer_recv.at[q], (me, sibling))

    half_count = cands // 2
    for d in range(1, half_count):
        to_peer(d).start()
    to_partner = remote(columns.at[y], columns.at[y], out_send.at[1 + half_count], out_recv, (partner, c))
    to_partner.start()
    to_sibling = remote(columns.at[y], peers.at[c], out_send.at[1], peer_recv.at[c], (me, sibling))
    to_sibling.start()
    peers[c] = columns[y]

    @pl.when(c != owner_cand)
    def _():
        remote(candidates, chosen, ch_send.at[0], ch_recv, (me, sibling)).wait_recv()

    points[...] = jnp.transpose(chosen[...] * scaling)
    within = pl.multiple_of((me * slab) % width, 8)
    covariance[...] = matern(points[pl.ds(within, slab), :], own_candidates[...] * scaling)

    for d in range(1, half_count):
        from_peer(lax.rem(c + 2 * d, cands)).wait_recv()
        pass_on(d).start()
    remote(columns.at[y], columns.at[1 - y], out_send.at[1], out_recv, (partner, c)).wait_recv()
    turned[...] = jnp.transpose(columns[...].reshape(width, pair))
    facing = split(turned[...])

    def piece_copy(q):
        group = 2 * q + y
        return remote(pieces.at[q], sums.at[z, group % ratio], sum_send.at[q],
                      sum_recv.at[z, group % ratio], (group // ratio, c))

    def piece(q):
        group = 2 * q + y
        pieces[q] = product(split(peers[q]), facing)

        @pl.when(group // ratio != me)
        def _():
            piece_copy(q).start()

        @pl.when(group // ratio == me)
        def _():
            sums[z, group % ratio] = pieces[q]

    piece(c)
    from_peer(sibling).wait_recv()
    piece(sibling)
    for d in range(1, half_count):
        piece(lax.rem(c + 2 * d, cands))
    for d in range(1, half_count):
        q = lax.rem(sibling + 2 * d, cands)
        from_peer(q).wait_recv()
        piece(q)

    whitened[...] = turned[pl.ds(pl.multiple_of(y * height, 8), height), :]

    for k in range(ratio):
        for step in range(steps):
            sender = 2 * step + lax.rem(ratio * me + k, 2)

            @pl.when(sender != me)
            def _(k=k, step=step):
                remote(pieces.at[0], sums.at[step, k], sum_send.at[0], sum_recv.at[step, k], (partner, c)).wait_recv()
        total = functools.reduce(jnp.add, [sums[step, k] for step in range(steps)])
        covariance[k * half:(k + 1) * half] = covariance[k * half:(k + 1) * half] - total

    @pl.when(c == owner_cand)
    def _():
        for d in range(1, cands):
            chosen_copy(d).wait_send()
    across(0).wait_send()
    beside(0).wait_send()

    @pl.when(y == 1)
    def _():
        across(1).wait_send()

    @pl.when(y == 0)
    def _():
        beside(1).wait_send()
    for j in range(steps - 1):
        @pl.when(z > j)
        def _(j=j):
            across(j + 2).wait_send()
            beside(j + 2).wait_send()
            if j < steps - 2:
                @pl.when(z < steps - 1)
                def _():
                    onward(j).wait_send()

        @pl.when(z == j)
        def _(j=j):
            launch(j).wait_send()
    for d in range(1, half_count):
        to_peer(d).wait_send()
        pass_on(d).wait_send()
    to_sibling.wait_send()
    to_partner.wait_send()
    for q in range(cands):
        @pl.when((2 * q + y) // ratio != me)
        def _(q=q):
            piece_copy(q).wait_send()


def shards(sections, cands, archive, candidates, lengths, factor):
    dims, height = archive.shape
    width = candidates.shape[1]
    pair, half, steps = 2 * height, width // 2, sections // 2
    ratio = (2 * cands) // sections
    vmem = pl.BlockSpec(memory_space=pltpu.VMEM)
    hbm = pl.BlockSpec(memory_space=pltpu.HBM)
    dma = pltpu.SemaphoreType.DMA
    return pl.pallas_call(
        functools.partial(kernel, sections, cands),
        out_shape=(jax.ShapeDtypeStruct((height, width), F32), jax.ShapeDtypeStruct((half * ratio, width), F32)),
        in_specs=[hbm] * 4,
        out_specs=(vmem, vmem),
        scratch_shapes=[
            pltpu.VMEM((2, dims, height), F32),
            pltpu.VMEM((2, height, pair), F32),
            pltpu.VMEM((steps - 1, 2, height, pair), F32),
            pltpu.VMEM((dims, width), F32),
            pltpu.VMEM((1, dims), F32),
            pltpu.VMEM((dims, width), F32),
            pltpu.VMEM((width, dims), F32),
            pltpu.VMEM((2, height, height), F32),
            pltpu.VMEM((steps - 1, pair, pair), jnp.bfloat16),
            pltpu.VMEM((steps - 1, pair, pair), jnp.bfloat16),
            pltpu.VMEM((steps - 1, half, pair), F32),
            pltpu.VMEM((cands, half, pair), F32),
            pltpu.VMEM((2, half, pair), F32),
            pltpu.VMEM((pair, width), F32),
            pltpu.VMEM((steps, ratio, half, width), F32),
            pltpu.VMEM((cands, half, width), F32),
            dma((4,)), dma((steps - 1,)),
            dma, dma,
            dma((cands - 1,)), dma,
            dma((steps + 1,)), dma((steps + 1,)), dma((steps + 1,)), dma((steps + 1,)),
            dma((steps - 1,)), dma((steps - 1,)),
            dma((2 + cands // 2,)), dma,
            dma((cands // 2,)), dma((cands,)),
            dma((cands,)), dma((steps, ratio)),
        ],
        compiler_params=pltpu.CompilerParams(
            collective_id=0, has_side_effects=True, vmem_limit_bytes=48 * 1024 * 1024),
    )(*(pltpu.with_memory_space_constraint(x, pltpu.HBM)
        for x in (archive, candidates, lengths.reshape(1, dims), factor)))


def solution(mesh):
    return jax.shard_map(
        functools.partial(shards, mesh.shape["chain"], mesh.shape["cand"]),
        mesh=mesh,
        in_specs=(P(None, "chain"), P(None, "cand"), P(), P("chain", None)),
        out_specs=(P("chain", "cand"), P("chain", "cand")),
        check_vma=False,
    )
```

```python
import functools
import jax
import jax.numpy as jnp
from jax import lax
from jax.experimental import pallas as pl
from jax.experimental.pallas import tpu as pltpu
from jax.sharding import PartitionSpec as P

MESH = pl.DeviceIdType.MESH
F32 = jnp.float32
BASE = 32
TILE = 128
CHUNKS = 2


def split(value):
    high = value.astype(jnp.bfloat16)
    return high, (value - high.astype(F32)).astype(jnp.bfloat16)


def product(first, second, transposed=False):
    dims = (((1,), (1 if transposed else 0,)), ((), ()))
    dot = functools.partial(lax.dot_general, dimension_numbers=dims, preferred_element_type=F32)
    return dot(first[0], second[0]) + (dot(first[0], second[1]) + dot(first[1], second[0]))


def matern(rows, columns):
    total = None
    for d in range(columns.shape[0]):
        differ = rows[:, d:d + 1] - columns[d:d + 1, :]
        total = differ * differ if total is None else total + differ * differ
    radius = jnp.sqrt(5.0 * total)
    return (1.0 + radius + radius * radius / 3.0) * jnp.exp(-radius)


def base_inverse(block):
    size = block.shape[0]
    count = size // BASE
    row = lax.broadcasted_iota(jnp.int32, (size, size), 0)
    column = lax.broadcasted_iota(jnp.int32, (size, size), 1)
    same = (row // BASE) == (column // BASE)
    kept = jnp.where(same, block, 0.0)
    packed = functools.reduce(jnp.add, [kept[b * BASE:(b + 1) * BASE] for b in range(count)])
    lane = lax.broadcasted_iota(jnp.int32, (BASE, size), 1) % BASE
    sub = lax.broadcasted_iota(jnp.int32, (BASE, size), 0)
    picked = jnp.concatenate([jnp.where(lane == k, packed, 0.0) for k in range(BASE)], axis=0)
    group = same.astype(F32).astype(jnp.bfloat16)
    spread = None
    rest = picked
    for _ in range(3):
        part = rest.astype(jnp.bfloat16)
        rest = rest - part.astype(F32)
        term = jnp.dot(part, group, preferred_element_type=F32)
        spread = term if spread is None else spread + term
    state = jnp.where(sub == lane, 1.0, 0.0).astype(F32)
    for k in range(BASE):
        coupling = spread[k * BASE:(k + 1) * BASE]
        solved = state[k:k + 1] * (1.0 / coupling[k:k + 1])
        state = jnp.where(sub == k, solved, jnp.where(sub > k, state - coupling * solved, state))
    return jnp.where(same, jnp.concatenate([state] * count, axis=0), 0.0)


def grow_inverse(block, inverse, start, end):
    size = block.shape[0]
    row = lax.broadcasted_iota(jnp.int32, (size, size), 0)
    column = lax.broadcasted_iota(jnp.int32, (size, size), 1)
    width = start
    while width < end:
        above = ((row // width) + 1 == (column // width)) & ((row // (2 * width)) == (column // (2 * width)))
        parts = split(inverse)
        middle = product(parts, split(jnp.where(above, block, 0.0)))
        inverse = inverse - product(split(middle), parts)
        width *= 2
    return inverse


def pack(upper):
    size = upper.shape[0]
    rest = upper[:, TILE:]
    beside = jnp.concatenate([rest[:size // 2], rest[size // 2:]], axis=1)
    return jnp.concatenate([upper[:TILE, :TILE], beside], axis=0)


def unpack(packed, size):
    beside = packed[TILE:]
    rest = jnp.concatenate([beside[:, :size - TILE], beside[:, size - TILE:]], axis=0)
    first = jnp.concatenate([packed[:TILE], jnp.zeros((size - TILE, TILE), F32)], axis=0)
    return jnp.concatenate([first, rest], axis=1)


def kernel(sections, cands, archive, candidates, lengths, factor, whitened, covariance,
           both_archive, near, far, own_candidates, own_lengths, chosen, points, inverses,
           high_weights, low_weights, panels, peers, columns, turned, sums, pieces,
           load, far_load, in_send, in_recv, ch_send, ch_recv, y_send, y_recv, s_send, s_recv,
           pan_send, pan_recv, out_send, out_recv, pass_send, peer_recv, sum_send, sum_recv):
    me = lax.axis_index("chain")
    c = lax.axis_index("cand")
    z, y = me // 2, me % 2
    steps = sections // 2
    core = c % 2
    height = factor.shape[0]
    pair = 2 * height
    cover = -(-height // 128) * 128
    width = candidates.shape[1]
    half = width // 2
    ratio = (2 * cands) // sections
    slab = half * ratio
    strip = height // 2
    partner = 2 * z + (1 - y)
    sibling = c + 1 - 2 * core
    mine = pl.ds(pl.multiple_of(core * strip, 8), strip)
    others = pl.ds(pl.multiple_of((1 - core) * strip, 8), strip)
    diagonal = pl.multiple_of(z * pair, 128)

    def remote(source, target, send, recv, where):
        return pltpu.make_async_remote_copy(
            src_ref=source, dst_ref=target, send_sem=send, recv_sem=recv, device_id=where, device_id_type=MESH)

    def far_copy(j):
        return pltpu.make_async_copy(factor.at[:, j * pair:(j + 1) * pair], far.at[j, y], far_load.at[j])

    near_copy = pltpu.make_async_copy(factor.at[:, pl.ds(diagonal, pair)], near.at[y], load.at[0])
    lengths_copy = pltpu.make_async_copy(lengths, own_lengths, load.at[1])
    candidates_copy = pltpu.make_async_copy(candidates, own_candidates, load.at[2])
    archive_copy = pltpu.make_async_copy(archive, both_archive.at[y], load.at[3])
    near_copy.start()
    lengths_copy.start()
    candidates_copy.start()
    archive_copy.start()

    barrier = pltpu.get_barrier_semaphore()
    for d in range(1, sections):
        pl.semaphore_signal(barrier, inc=1, device_id=(lax.rem(me + d, sections), c), device_id_type=MESH)
    for d in range(1, cands):
        pl.semaphore_signal(barrier, inc=1, device_id=(me, lax.rem(c + d, cands)), device_id_type=MESH)
    for j in range(steps - 1):
        @pl.when(z > j)
        def _(j=j):
            far_copy(j).start()

    near_copy.wait()
    strip_of_pair = near[y]
    block = jnp.where(y == 0, strip_of_pair[:, :height], strip_of_pair[:, height:])
    small = jnp.transpose(base_inverse(block))
    block = jnp.transpose(block)
    small = grow_inverse(block, small, BASE, 2 * BASE)
    lengths_copy.wait()
    candidates_copy.wait()
    archive_copy.wait()
    scale_row = 1.0 / own_lengths[...]
    scaling = jnp.transpose(jnp.broadcast_to(scale_row, (8, scale_row.shape[1])))[:, :1]
    owner_cand = (me * slab) // width

    pl.semaphore_wait(barrier, sections + cands - 2)

    send_in = remote(archive, both_archive.at[y], in_send, in_recv, (partner, c))
    send_in.start()

    def area(e, who, rows):
        if e == 1:
            return near.at[1, rows, pl.ds(0, cover)]
        return far.at[e - 2, who, rows]

    def across(e):
        if e == 0:
            return remote(inverses.at[y], inverses.at[y], y_send.at[e], y_recv.at[e], (partner, c))
        if e == 1:
            source = factor.at[mine, pl.ds(diagonal, cover)]
        else:
            source = factor.at[mine, pl.ds((e - 2) * pair, pair)]
        return remote(source, area(e, y, mine), y_send.at[e], y_recv.at[e], (partner, c))

    def across_recv(e):
        if e == 0:
            return remote(inverses.at[1 - y], inverses.at[1 - y], y_send.at[e], y_recv.at[e], (partner, c))
        return remote(area(e, 1 - y, mine), area(e, 1 - y, mine), y_send.at[e], y_recv.at[e], (partner, c))

    def beside(e):
        return remote(area(e, 1 - y, mine), area(e, 1 - y, mine), s_send.at[e], s_recv.at[e], (me, sibling))

    def beside_recv(e):
        return remote(area(e, 1 - y, others), area(e, 1 - y, others), s_send.at[e], s_recv.at[e], (me, sibling))

    @pl.when(y == 1)
    def _():
        across(1).start()
    early = min(2, steps - 1)
    for j in range(early):
        @pl.when(z > j)
        def _(j=j):
            across(j + 2).start()

    def chosen_copy(d):
        return remote(candidates, chosen, ch_send.at[d - 1], ch_recv, (me, lax.rem(c + d, cands)))

    @pl.when(c == owner_cand)
    def _():
        for d in range(1, cands):
            chosen_copy(d).start()
        chosen[...] = own_candidates[...]

    inverses[y] = pack(grow_inverse(block, small, 2 * BASE, height))
    across(0).start()
    for j in range(early, steps - 1):
        @pl.when(z > j)
        def _(j=j):
            across(j + 2).start()

    @pl.when(y == 0)
    def _():
        across_recv(1).wait_recv()
        beside(1).start()

    points[...] = jnp.transpose(own_candidates[...] * scaling)
    own_points = points[pl.ds(pl.multiple_of(y * half, 8), half), :]
    send_in.wait_send()
    remote(archive, both_archive.at[1 - y], in_send, in_recv, (partner, c)).wait_recv()
    upper_cross = split(matern(own_points, both_archive[0] * scaling))
    lower_cross = split(matern(own_points, both_archive[1] * scaling))

    @pl.when(y == 0)
    def _():
        beside_recv(1).wait_recv()

    coupling = split(jnp.transpose(near[1][:, :height]))

    def pass_far(j):
        far_copy(j).wait()
        across_recv(j + 2).wait_recv()
        beside(j + 2).start()

    def turn_far(j):
        beside_recv(j + 2).wait_recv()
        high, low = split(jnp.transpose(far[j].reshape(pair, pair)))
        high_weights[j] = high
        low_weights[j] = low

    for j in range(early):
        @pl.when(z > j)
        def _(j=j):
            pass_far(j)
    for j in range(early):
        @pl.when(z > j)
        def _(j=j):
            turn_far(j)
    across_recv(0).wait_recv()
    upper_inverse = unpack(inverses[0], height)
    lower_inverse = unpack(inverses[1], height)
    upper = split(upper_inverse)
    lower = split(lower_inverse)
    between = split(product(coupling, lower))
    part = half // CHUNKS
    half_count = cands // 2

    def rows_of(k):
        return pl.ds(k * part, part)

    def launch(j, k):
        return remote(columns.at[y, rows_of(k)], panels.at[j, rows_of(k)], out_send.at[0, k], pan_recv.at[j, k],
                      (lax.rem(me + 2, sections), c))

    def to_peer(d, k):
        return remote(columns.at[y, rows_of(k)], peers.at[c, rows_of(k)], out_send.at[1 + d, k], peer_recv.at[c, k],
                      (me, lax.rem(c + 2 * d, cands)))

    def to_sibling(k):
        return remote(columns.at[y, rows_of(k)], peers.at[c, rows_of(k)], out_send.at[1, k], peer_recv.at[c, k],
                      (me, sibling))

    def to_partner(k):
        return remote(columns.at[y, rows_of(k)], columns.at[y, rows_of(k)], out_send.at[1 + half_count, k],
                      out_recv.at[k], (partner, c))

    def emit(j, k):
        if j < steps - 1:
            launch(j, k).start()
        for d in range(1, half_count):
            to_peer(d, k).start()
        to_partner(k).start()
        to_sibling(k).start()

    for k in range(CHUNKS):
        rows = slice(k * part, (k + 1) * part)
        first = product([p[rows] for p in upper_cross], upper)
        second = product([p[rows] for p in lower_cross], lower) - product(split(first), between)
        columns[y, rows] = jnp.concatenate([first, second], axis=1)

        @pl.when(z == 0)
        def _(k=k):
            emit(0, k)

    @pl.when(z > 0)
    def _():
        corner = -product(upper, between)
        whole = split(jnp.concatenate([
            jnp.concatenate([upper_inverse, corner], axis=1),
            jnp.concatenate([jnp.zeros((height, height), F32), lower_inverse], axis=1)], axis=0))
        for j in range(steps - 1):
            @pl.when(z > j)
            def _(j=j):
                if j >= early:
                    pass_far(j)
                    turn_far(j)
                weights = product((high_weights[j], low_weights[j]), whole)
                high, low = split(weights)
                high_weights[j] = high
                low_weights[j] = low

    def onward(j, k):
        return remote(panels.at[j, rows_of(k)], panels.at[j, rows_of(k)], pan_send.at[j, k], pan_recv.at[j, k],
                      (lax.rem(me + 2, sections), c))

    for j in range(steps - 1):
        @pl.when(z > j)
        def _(j=j):
            for k in range(CHUNKS):
                onward(j, k).wait_recv()
                if j < steps - 2:
                    @pl.when(z < steps - 1)
                    def _():
                        onward(j, k).start()
                rows = slice(k * part, (k + 1) * part)
                columns[y, rows] = columns[y, rows] - product(
                    split(panels[j, rows]), (high_weights[j], low_weights[j]))

                @pl.when(z == j + 1)
                def _():
                    emit(j + 1, k)

    def from_peer(q, k):
        return remote(columns.at[y, rows_of(k)], peers.at[q, rows_of(k)], out_send.at[1, k], peer_recv.at[q, k],
                      (me, sibling))

    def pass_on(d, k):
        q = lax.rem(c + 2 * d, cands)
        return remote(peers.at[q, rows_of(k)], peers.at[q, rows_of(k)], pass_send.at[d, k], peer_recv.at[q, k],
                      (me, sibling))

    def wait_peer(q):
        for k in range(CHUNKS):
            from_peer(q, k).wait_recv()

    peers[c] = columns[y]

    @pl.when(c != owner_cand)
    def _():
        remote(candidates, chosen, ch_send.at[0], ch_recv, (me, sibling)).wait_recv()

    points[...] = jnp.transpose(chosen[...] * scaling)
    within = pl.multiple_of((me * slab) % width, 8)
    covariance[...] = matern(points[pl.ds(within, slab), :], own_candidates[...] * scaling)

    for k in range(CHUNKS):
        for d in range(1, half_count):
            from_peer(lax.rem(c + 2 * d, cands), k).wait_recv()
            pass_on(d, k).start()
    for k in range(CHUNKS):
        remote(columns.at[y, rows_of(k)], columns.at[1 - y, rows_of(k)], out_send.at[1, k], out_recv.at[k],
               (partner, c)).wait_recv()
    turned[...] = jnp.transpose(columns[...].reshape(width, pair))
    facing = split(turned[...])

    def piece_copy(q):
        group = 2 * q + y
        return remote(pieces.at[q], sums.at[z, group % ratio], sum_send.at[q],
                      sum_recv.at[z, group % ratio], (group // ratio, c))

    def piece(q):
        group = 2 * q + y
        pieces[q] = product(split(peers[q]), facing)

        @pl.when(group // ratio != me)
        def _():
            piece_copy(q).start()

        @pl.when(group // ratio == me)
        def _():
            sums[z, group % ratio] = pieces[q]

    piece(c)
    wait_peer(sibling)
    piece(sibling)
    for d in range(1, half_count):
        piece(lax.rem(c + 2 * d, cands))
    for d in range(1, half_count):
        q = lax.rem(sibling + 2 * d, cands)
        wait_peer(q)
        piece(q)

    whitened[...] = turned[pl.ds(pl.multiple_of(y * height, 8), height), :]

    for k in range(ratio):
        for step in range(steps):
            sender = 2 * step + lax.rem(ratio * me + k, 2)

            @pl.when(sender != me)
            def _(k=k, step=step):
                remote(pieces.at[0], sums.at[step, k], sum_send.at[0], sum_recv.at[step, k], (partner, c)).wait_recv()
        total = functools.reduce(jnp.add, [sums[step, k] for step in range(steps)])
        covariance[k * half:(k + 1) * half] = covariance[k * half:(k + 1) * half] - total

    @pl.when(c == owner_cand)
    def _():
        for d in range(1, cands):
            chosen_copy(d).wait_send()
    across(0).wait_send()

    @pl.when(y == 1)
    def _():
        across(1).wait_send()

    @pl.when(y == 0)
    def _():
        beside(1).wait_send()
    for j in range(steps - 1):
        @pl.when(z > j)
        def _(j=j):
            across(j + 2).wait_send()
            beside(j + 2).wait_send()
            if j < steps - 2:
                @pl.when(z < steps - 1)
                def _():
                    for k in range(CHUNKS):
                        onward(j, k).wait_send()

        @pl.when(z == j)
        def _(j=j):
            for k in range(CHUNKS):
                launch(j, k).wait_send()
    for k in range(CHUNKS):
        for d in range(1, half_count):
            to_peer(d, k).wait_send()
            pass_on(d, k).wait_send()
        to_sibling(k).wait_send()
        to_partner(k).wait_send()
    for q in range(cands):
        @pl.when((2 * q + y) // ratio != me)
        def _(q=q):
            piece_copy(q).wait_send()


def shards(sections, cands, archive, candidates, lengths, factor):
    dims, height = archive.shape
    width = candidates.shape[1]
    pair, half, steps = 2 * height, width // 2, sections // 2
    ratio = (2 * cands) // sections
    vmem = pl.BlockSpec(memory_space=pltpu.VMEM)
    hbm = pl.BlockSpec(memory_space=pltpu.HBM)
    dma = pltpu.SemaphoreType.DMA
    return pl.pallas_call(
        functools.partial(kernel, sections, cands),
        out_shape=(jax.ShapeDtypeStruct((height, width), F32), jax.ShapeDtypeStruct((half * ratio, width), F32)),
        in_specs=[hbm] * 4,
        out_specs=(vmem, vmem),
        scratch_shapes=[
            pltpu.VMEM((2, dims, height), F32),
            pltpu.VMEM((2, height, pair), F32),
            pltpu.VMEM((steps - 1, 2, height, pair), F32),
            pltpu.VMEM((dims, width), F32),
            pltpu.VMEM((1, dims), F32),
            pltpu.VMEM((dims, width), F32),
            pltpu.VMEM((width, dims), F32),
            pltpu.VMEM((2, TILE + height // 2, TILE), F32),
            pltpu.VMEM((steps - 1, pair, pair), jnp.bfloat16),
            pltpu.VMEM((steps - 1, pair, pair), jnp.bfloat16),
            pltpu.VMEM((steps - 1, half, pair), F32),
            pltpu.VMEM((cands, half, pair), F32),
            pltpu.VMEM((2, half, pair), F32),
            pltpu.VMEM((pair, width), F32),
            pltpu.VMEM((steps, ratio, half, width), F32),
            pltpu.VMEM((cands, half, width), F32),
            dma((4,)), dma((steps - 1,)),
            dma, dma,
            dma((cands - 1,)), dma,
            dma((steps + 1,)), dma((steps + 1,)), dma((steps + 1,)), dma((steps + 1,)),
            dma((steps - 1, CHUNKS)), dma((steps - 1, CHUNKS)),
            dma((2 + cands // 2, CHUNKS)), dma((CHUNKS,)),
            dma((cands // 2, CHUNKS)), dma((cands, CHUNKS)),
            dma((cands,)), dma((steps, ratio)),
        ],
        compiler_params=pltpu.CompilerParams(
            collective_id=0, has_side_effects=True, vmem_limit_bytes=48 * 1024 * 1024),
    )(*(pltpu.with_memory_space_constraint(x, pltpu.HBM)
        for x in (archive, candidates, lengths.reshape(1, dims), factor)))


def solution(mesh):
    return jax.shard_map(
        functools.partial(shards, mesh.shape["chain"], mesh.shape["cand"]),
        mesh=mesh,
        in_specs=(P(None, "chain"), P(None, "cand"), P(), P("chain", None)),
        out_specs=(P("chain", "cand"), P("chain", "cand")),
        check_vma=False,
    )
```

```python
import functools
import jax
import jax.numpy as jnp
from jax import lax
from jax.experimental import pallas as pl
from jax.experimental.pallas import tpu as pltpu
from jax.sharding import PartitionSpec as P

MESH = pl.DeviceIdType.MESH
F32 = jnp.float32
BASE = 32
TILE = 128
CHUNKS = 2


def split(value):
    high = value.astype(jnp.bfloat16)
    return high, (value - high.astype(F32)).astype(jnp.bfloat16)


def product(first, second, transposed=False):
    dims = (((1,), (1 if transposed else 0,)), ((), ()))
    dot = functools.partial(lax.dot_general, dimension_numbers=dims, preferred_element_type=F32)
    return dot(first[0], second[0]) + (dot(first[0], second[1]) + dot(first[1], second[0]))


def matern(rows, columns):
    total = None
    for d in range(columns.shape[0]):
        differ = rows[:, d:d + 1] - columns[d:d + 1, :]
        total = differ * differ if total is None else total + differ * differ
    radius = jnp.sqrt(5.0 * total)
    return (1.0 + radius + radius * radius / 3.0) * jnp.exp(-radius)


def base_inverse(block):
    size = block.shape[0]
    count = size // BASE
    row = lax.broadcasted_iota(jnp.int32, (size, size), 0)
    column = lax.broadcasted_iota(jnp.int32, (size, size), 1)
    same = (row // BASE) == (column // BASE)
    kept = jnp.where(same, block, 0.0)
    packed = functools.reduce(jnp.add, [kept[b * BASE:(b + 1) * BASE] for b in range(count)])
    lane = lax.broadcasted_iota(jnp.int32, (BASE, size), 1) % BASE
    sub = lax.broadcasted_iota(jnp.int32, (BASE, size), 0)
    picked = jnp.concatenate([jnp.where(lane == k, packed, 0.0) for k in range(BASE)], axis=0)
    group = same.astype(F32).astype(jnp.bfloat16)
    spread = None
    rest = picked
    for _ in range(3):
        part = rest.astype(jnp.bfloat16)
        rest = rest - part.astype(F32)
        term = jnp.dot(part, group, preferred_element_type=F32)
        spread = term if spread is None else spread + term
    state = jnp.where(sub == lane, 1.0, 0.0).astype(F32)
    for k in range(BASE):
        coupling = spread[k * BASE:(k + 1) * BASE]
        solved = state[k:k + 1] * (1.0 / coupling[k:k + 1])
        state = jnp.where(sub == k, solved, jnp.where(sub > k, state - coupling * solved, state))
    return jnp.where(same, jnp.concatenate([state] * count, axis=0), 0.0)


def grow_inverse(block, inverse, start, end):
    size = block.shape[0]
    row = lax.broadcasted_iota(jnp.int32, (size, size), 0)
    column = lax.broadcasted_iota(jnp.int32, (size, size), 1)
    width = start
    while width < end:
        above = ((row // width) + 1 == (column // width)) & ((row // (2 * width)) == (column // (2 * width)))
        parts = split(inverse)
        middle = product(parts, split(jnp.where(above, block, 0.0)))
        inverse = inverse - product(split(middle), parts)
        width *= 2
    return inverse


def pack(upper):
    size = upper.shape[0]
    rest = upper[:, TILE:]
    beside = jnp.concatenate([rest[:size // 2], rest[size // 2:]], axis=1)
    return jnp.concatenate([upper[:TILE, :TILE], beside], axis=0)


def unpack(packed, size):
    beside = packed[TILE:]
    rest = jnp.concatenate([beside[:, :size - TILE], beside[:, size - TILE:]], axis=0)
    first = jnp.concatenate([packed[:TILE], jnp.zeros((size - TILE, TILE), F32)], axis=0)
    return jnp.concatenate([first, rest], axis=1)


def kernel(sections, cands, archive, candidates, lengths, factor, whitened, covariance,
           both_archive, near, far, own_candidates, own_lengths, chosen, points, inverses,
           high_weights, low_weights, panels, peers, columns, turned, sums, pieces,
           load, far_load, in_send, in_recv, ch_send, ch_recv, y_send, y_recv, s_send, s_recv,
           pan_send, pan_recv, out_send, out_recv, pass_send, peer_recv, sum_send, sum_recv, ready):
    me = lax.axis_index("chain")
    c = lax.axis_index("cand")
    z, y = me // 2, me % 2
    steps = sections // 2
    core = c % 2
    height = factor.shape[0]
    pair = 2 * height
    cover = -(-height // 128) * 128
    width = candidates.shape[1]
    half = width // 2
    ratio = (2 * cands) // sections
    slab = half * ratio
    strip = height // 2
    partner = 2 * z + (1 - y)
    sibling = c + 1 - 2 * core
    mine = pl.ds(pl.multiple_of(core * strip, 8), strip)
    others = pl.ds(pl.multiple_of((1 - core) * strip, 8), strip)
    diagonal = pl.multiple_of(z * pair, 128)

    def remote(source, target, send, recv, where):
        return pltpu.make_async_remote_copy(
            src_ref=source, dst_ref=target, send_sem=send, recv_sem=recv, device_id=where, device_id_type=MESH)

    def far_copy(j):
        return pltpu.make_async_copy(factor.at[:, j * pair:(j + 1) * pair], far.at[j, y], far_load.at[j])

    near_copy = pltpu.make_async_copy(factor.at[:, pl.ds(diagonal, pair)], near.at[y], load.at[0])
    lengths_copy = pltpu.make_async_copy(lengths, own_lengths, load.at[1])
    candidates_copy = pltpu.make_async_copy(candidates, own_candidates, load.at[2])
    archive_copy = pltpu.make_async_copy(archive, both_archive.at[y], load.at[3])
    near_copy.start()
    lengths_copy.start()
    candidates_copy.start()
    archive_copy.start()

    barrier = pltpu.get_barrier_semaphore()
    pl.semaphore_signal(barrier, inc=1, device_id=(partner, c), device_id_type=MESH)

    @pl.when(z > 0)
    def _():
        pl.semaphore_signal(barrier, inc=1, device_id=(lax.rem(me + sections - 2, sections), c), device_id_type=MESH)

    @pl.when(z < steps - 1)
    def _():
        pl.semaphore_signal(barrier, inc=1, device_id=(lax.rem(me + 2, sections), c), device_id_type=MESH)
    for d in range(1, cands):
        pl.semaphore_signal(barrier, inc=1, device_id=(me, lax.rem(c + d, cands)), device_id_type=MESH)
    for j in range(steps - 1):
        @pl.when(z > j)
        def _(j=j):
            far_copy(j).start()

    near_copy.wait()
    strip_of_pair = near[y]
    block = jnp.where(y == 0, strip_of_pair[:, :height], strip_of_pair[:, height:])
    small = jnp.transpose(base_inverse(block))
    block = jnp.transpose(block)
    small = grow_inverse(block, small, BASE, 2 * BASE)
    lengths_copy.wait()
    candidates_copy.wait()
    archive_copy.wait()
    scale_row = 1.0 / own_lengths[...]
    scaling = jnp.transpose(jnp.broadcast_to(scale_row, (8, scale_row.shape[1])))[:, :1]
    owner_cand = (me * slab) // width

    neighbours = cands + jnp.where(z > 0, 1, 0) + jnp.where(z < steps - 1, 1, 0)
    pl.semaphore_wait(barrier, neighbours)

    send_in = remote(archive, both_archive.at[y], in_send, in_recv, (partner, c))
    send_in.start()

    def area(e, who, rows):
        if e == 1:
            return near.at[1, rows, pl.ds(0, cover)]
        return far.at[e - 2, who, rows]

    def across(e):
        if e == 0:
            return remote(inverses.at[y], inverses.at[y], y_send.at[e], y_recv.at[e], (partner, c))
        if e == 1:
            source = factor.at[mine, pl.ds(diagonal, cover)]
        else:
            source = factor.at[mine, pl.ds((e - 2) * pair, pair)]
        return remote(source, area(e, y, mine), y_send.at[e], y_recv.at[e], (partner, c))

    def across_recv(e):
        if e == 0:
            return remote(inverses.at[1 - y], inverses.at[1 - y], y_send.at[e], y_recv.at[e], (partner, c))
        return remote(area(e, 1 - y, mine), area(e, 1 - y, mine), y_send.at[e], y_recv.at[e], (partner, c))

    def beside(e):
        return remote(area(e, 1 - y, mine), area(e, 1 - y, mine), s_send.at[e], s_recv.at[e], (me, sibling))

    def beside_recv(e):
        return remote(area(e, 1 - y, others), area(e, 1 - y, others), s_send.at[e], s_recv.at[e], (me, sibling))

    @pl.when(y == 1)
    def _():
        across(1).start()
    early = min(2, steps - 1)
    for j in range(early):
        @pl.when(z > j)
        def _(j=j):
            across(j + 2).start()

    def chosen_copy(d):
        return remote(candidates, chosen, ch_send.at[d - 1], ch_recv, (me, lax.rem(c + d, cands)))

    @pl.when(c == owner_cand)
    def _():
        for d in range(1, cands):
            chosen_copy(d).start()
        chosen[...] = own_candidates[...]

    inverses[y] = pack(grow_inverse(block, small, 2 * BASE, height))
    across(0).start()
    for j in range(early, steps - 1):
        @pl.when(z > j)
        def _(j=j):
            across(j + 2).start()

    @pl.when(y == 0)
    def _():
        across_recv(1).wait_recv()
        beside(1).start()

    points[...] = jnp.transpose(own_candidates[...] * scaling)
    own_points = points[pl.ds(pl.multiple_of(y * half, 8), half), :]
    send_in.wait_send()
    remote(archive, both_archive.at[1 - y], in_send, in_recv, (partner, c)).wait_recv()
    cross = jnp.concatenate(
        [matern(own_points, both_archive[0] * scaling), matern(own_points, both_archive[1] * scaling)], axis=1)
    columns[y] = cross

    @pl.when(y == 0)
    def _():
        beside_recv(1).wait_recv()

    coupling = split(jnp.transpose(near[1][:, :height]))

    def pass_far(j):
        far_copy(j).wait()
        across_recv(j + 2).wait_recv()
        beside(j + 2).start()

    def turn_far(j):
        beside_recv(j + 2).wait_recv()
        high, low = split(jnp.transpose(far[j].reshape(pair, pair)))
        high_weights[j] = high
        low_weights[j] = low

    for j in range(early):
        @pl.when(z > j)
        def _(j=j):
            pass_far(j)
    for j in range(early):
        @pl.when(z > j)
        def _(j=j):
            turn_far(j)
    @pl.when((z > 0) & (z < steps - 1))
    def _():
        pl.semaphore_wait(ready, 1)

    @pl.when(z > 0)
    def _():
        pl.semaphore_signal(ready, inc=1, device_id=(lax.rem(me + sections - 2, sections), c), device_id_type=MESH)

    across_recv(0).wait_recv()
    upper_inverse = unpack(inverses[0], height)
    lower_inverse = unpack(inverses[1], height)
    upper = split(upper_inverse)
    lower = split(lower_inverse)
    between = split(product(coupling, lower))
    part = half // CHUNKS
    half_count = cands // 2

    def rows_of(k):
        return pl.ds(k * part, part)

    def launch(j, k):
        return remote(columns.at[y, rows_of(k)], panels.at[j, rows_of(k)], out_send.at[0, k], pan_recv.at[j, k],
                      (lax.rem(me + 2, sections), c))

    def to_peer(d, k):
        return remote(columns.at[y, rows_of(k)], peers.at[c, rows_of(k)], out_send.at[1 + d, k], peer_recv.at[c, k],
                      (me, lax.rem(c + 2 * d, cands)))

    def to_sibling(k):
        return remote(columns.at[y, rows_of(k)], peers.at[c, rows_of(k)], out_send.at[1, k], peer_recv.at[c, k],
                      (me, sibling))

    def to_partner(k):
        return remote(columns.at[y, rows_of(k)], columns.at[y, rows_of(k)], out_send.at[1 + half_count, k],
                      out_recv.at[k], (partner, c))

    def emit(j, k):
        if j < steps - 1:
            launch(j, k).start()
        for d in range(1, half_count):
            to_peer(d, k).start()
        to_partner(k).start()
        to_sibling(k).start()

    def solve(k):
        rows = slice(k * part, (k + 1) * part)
        residue = columns[y, rows]
        first = product(split(residue[:, :height]), upper)
        second = product(split(residue[:, height:]), lower) - product(split(first), between)
        columns[y, rows] = jnp.concatenate([first, second], axis=1)

    @pl.when(z == 0)
    def _():
        for k in range(CHUNKS):
            solve(k)
            emit(0, k)

    def onward(j, k):
        return remote(panels.at[j, rows_of(k)], panels.at[j, rows_of(k)], pan_send.at[j, k], pan_recv.at[j, k],
                      (lax.rem(me + 2, sections), c))

    def subtract(j, k, weights):
        onward(j, k).wait_recv()
        if j < steps - 2:
            @pl.when(z < steps - 1)
            def _():
                onward(j, k).start()
        rows = slice(k * part, (k + 1) * part)
        columns[y, rows] = columns[y, rows] - product(split(panels[j, rows]), weights)

    @pl.when(z > 0)
    def _():
        corner = -product(upper, between)
        whole = split(jnp.concatenate([
            jnp.concatenate([upper_inverse, corner], axis=1),
            jnp.concatenate([jnp.zeros((height, height), F32), lower_inverse], axis=1)], axis=0))
        for j in range(early, steps - 1):
            @pl.when(z > j)
            def _(j=j):
                pass_far(j)
                turn_far(j)
        for j in range(steps - 1):
            @pl.when(z == j + 1)
            def _(j=j):
                high, low = split(product((high_weights[j], low_weights[j]), whole))
                high_weights[j] = high
                low_weights[j] = low
        for j in range(steps - 2):
            @pl.when(z > j + 1)
            def _(j=j):
                for k in range(CHUNKS):
                    subtract(j, k, (high_weights[j], low_weights[j]))
        for k in range(CHUNKS):
            solve(k)
        for j in range(steps - 1):
            @pl.when(z == j + 1)
            def _(j=j):
                for k in range(CHUNKS):
                    subtract(j, k, (high_weights[j], low_weights[j]))
                    emit(j + 1, k)

    def from_peer(q, k):
        return remote(columns.at[y, rows_of(k)], peers.at[q, rows_of(k)], out_send.at[1, k], peer_recv.at[q, k],
                      (me, sibling))

    def pass_on(d, k):
        q = lax.rem(c + 2 * d, cands)
        return remote(peers.at[q, rows_of(k)], peers.at[q, rows_of(k)], pass_send.at[d, k], peer_recv.at[q, k],
                      (me, sibling))

    def wait_peer(q):
        for k in range(CHUNKS):
            from_peer(q, k).wait_recv()

    peers[c] = columns[y]

    @pl.when(c != owner_cand)
    def _():
        remote(candidates, chosen, ch_send.at[0], ch_recv, (me, sibling)).wait_recv()

    points[...] = jnp.transpose(chosen[...] * scaling)
    within = pl.multiple_of((me * slab) % width, 8)
    covariance[...] = matern(points[pl.ds(within, slab), :], own_candidates[...] * scaling)

    for k in range(CHUNKS):
        for d in range(1, half_count):
            from_peer(lax.rem(c + 2 * d, cands), k).wait_recv()
            pass_on(d, k).start()
    for k in range(CHUNKS):
        remote(columns.at[y, rows_of(k)], columns.at[1 - y, rows_of(k)], out_send.at[1, k], out_recv.at[k],
               (partner, c)).wait_recv()
    turned[...] = jnp.transpose(columns[...].reshape(width, pair))
    facing = split(turned[...])

    def piece_copy(q):
        group = 2 * q + y
        return remote(pieces.at[q], sums.at[z, group % ratio], sum_send.at[q],
                      sum_recv.at[z, group % ratio], (group // ratio, c))

    def piece(q):
        group = 2 * q + y
        pieces[q] = product(split(peers[q]), facing)

        @pl.when(group // ratio != me)
        def _():
            piece_copy(q).start()

        @pl.when(group // ratio == me)
        def _():
            sums[z, group % ratio] = pieces[q]

    @pl.when(z == 0)
    def _():
        pl.semaphore_wait(ready, 1)

    piece(c)
    wait_peer(sibling)
    piece(sibling)
    for d in range(1, half_count):
        piece(lax.rem(c + 2 * d, cands))
    for d in range(1, half_count):
        q = lax.rem(sibling + 2 * d, cands)
        wait_peer(q)
        piece(q)

    whitened[...] = turned[pl.ds(pl.multiple_of(y * height, 8), height), :]

    for k in range(ratio):
        for step in range(steps):
            sender = 2 * step + lax.rem(ratio * me + k, 2)

            @pl.when(sender != me)
            def _(k=k, step=step):
                remote(pieces.at[0], sums.at[step, k], sum_send.at[0], sum_recv.at[step, k], (partner, c)).wait_recv()
        total = functools.reduce(jnp.add, [sums[step, k] for step in range(steps)])
        covariance[k * half:(k + 1) * half] = covariance[k * half:(k + 1) * half] - total

    @pl.when(c == owner_cand)
    def _():
        for d in range(1, cands):
            chosen_copy(d).wait_send()
    across(0).wait_send()

    @pl.when(y == 1)
    def _():
        across(1).wait_send()

    @pl.when(y == 0)
    def _():
        beside(1).wait_send()
    for j in range(steps - 1):
        @pl.when(z > j)
        def _(j=j):
            across(j + 2).wait_send()
            beside(j + 2).wait_send()
            if j < steps - 2:
                @pl.when(z < steps - 1)
                def _():
                    for k in range(CHUNKS):
                        onward(j, k).wait_send()

        @pl.when(z == j)
        def _(j=j):
            for k in range(CHUNKS):
                launch(j, k).wait_send()
    for k in range(CHUNKS):
        for d in range(1, half_count):
            to_peer(d, k).wait_send()
            pass_on(d, k).wait_send()
        to_sibling(k).wait_send()
        to_partner(k).wait_send()
    for q in range(cands):
        @pl.when((2 * q + y) // ratio != me)
        def _(q=q):
            piece_copy(q).wait_send()


def shards(sections, cands, archive, candidates, lengths, factor):
    dims, height = archive.shape
    width = candidates.shape[1]
    pair, half, steps = 2 * height, width // 2, sections // 2
    ratio = (2 * cands) // sections
    vmem = pl.BlockSpec(memory_space=pltpu.VMEM)
    hbm = pl.BlockSpec(memory_space=pltpu.HBM)
    dma = pltpu.SemaphoreType.DMA
    return pl.pallas_call(
        functools.partial(kernel, sections, cands),
        out_shape=(jax.ShapeDtypeStruct((height, width), F32), jax.ShapeDtypeStruct((half * ratio, width), F32)),
        in_specs=[hbm] * 4,
        out_specs=(vmem, vmem),
        scratch_shapes=[
            pltpu.VMEM((2, dims, height), F32),
            pltpu.VMEM((2, height, pair), F32),
            pltpu.VMEM((steps - 1, 2, height, pair), F32),
            pltpu.VMEM((dims, width), F32),
            pltpu.VMEM((1, dims), F32),
            pltpu.VMEM((dims, width), F32),
            pltpu.VMEM((width, dims), F32),
            pltpu.VMEM((2, TILE + height // 2, TILE), F32),
            pltpu.VMEM((steps - 1, pair, pair), jnp.bfloat16),
            pltpu.VMEM((steps - 1, pair, pair), jnp.bfloat16),
            pltpu.VMEM((steps - 1, half, pair), F32),
            pltpu.VMEM((cands, half, pair), F32),
            pltpu.VMEM((2, half, pair), F32),
            pltpu.VMEM((pair, width), F32),
            pltpu.VMEM((steps, ratio, half, width), F32),
            pltpu.VMEM((cands, half, width), F32),
            dma((4,)), dma((steps - 1,)),
            dma, dma,
            dma((cands - 1,)), dma,
            dma((steps + 1,)), dma((steps + 1,)), dma((steps + 1,)), dma((steps + 1,)),
            dma((steps - 1, CHUNKS)), dma((steps - 1, CHUNKS)),
            dma((2 + cands // 2, CHUNKS)), dma((CHUNKS,)),
            dma((cands // 2, CHUNKS)), dma((cands, CHUNKS)),
            dma((cands,)), dma((steps, ratio)),
            pltpu.SemaphoreType.REGULAR,
        ],
        compiler_params=pltpu.CompilerParams(
            collective_id=0, has_side_effects=True, vmem_limit_bytes=48 * 1024 * 1024),
    )(*(pltpu.with_memory_space_constraint(x, pltpu.HBM)
        for x in (archive, candidates, lengths.reshape(1, dims), factor)))


def solution(mesh):
    return jax.shard_map(
        functools.partial(shards, mesh.shape["chain"], mesh.shape["cand"]),
        mesh=mesh,
        in_specs=(P(None, "chain"), P(None, "cand"), P(), P("chain", None)),
        out_specs=(P("chain", "cand"), P("chain", "cand")),
        check_vma=False,
    )
```

```python
import functools
import jax
import jax.numpy as jnp
from jax import lax
from jax.experimental import pallas as pl
from jax.experimental.pallas import tpu as pltpu
from jax.sharding import PartitionSpec as P

MESH = pl.DeviceIdType.MESH
F32 = jnp.float32
BASE = 32
TILE = 128
CHUNKS = 2


def split(value):
    high = value.astype(jnp.bfloat16)
    return high, (value - high.astype(F32)).astype(jnp.bfloat16)


def product(first, second, transposed=False):
    dims = (((1,), (1 if transposed else 0,)), ((), ()))
    dot = functools.partial(lax.dot_general, dimension_numbers=dims, preferred_element_type=F32)
    count = first[0].shape[0]
    stacked = dot(jnp.concatenate([first[0], first[1]], axis=0), second[0])
    return stacked[:count] + (stacked[count:] + dot(first[0], second[1]))


def matern(rows, columns):
    total = None
    for d in range(columns.shape[0]):
        differ = rows[:, d:d + 1] - columns[d:d + 1, :]
        total = differ * differ if total is None else total + differ * differ
    radius = jnp.sqrt(5.0 * total)
    return (1.0 + radius + radius * radius / 3.0) * jnp.exp(-radius)


def base_inverse(block):
    size = block.shape[0]
    count = size // BASE
    row = lax.broadcasted_iota(jnp.int32, (size, size), 0)
    column = lax.broadcasted_iota(jnp.int32, (size, size), 1)
    same = (row // BASE) == (column // BASE)
    kept = jnp.where(same, block, 0.0)
    packed = functools.reduce(jnp.add, [kept[b * BASE:(b + 1) * BASE] for b in range(count)])
    lane = lax.broadcasted_iota(jnp.int32, (BASE, size), 1) % BASE
    sub = lax.broadcasted_iota(jnp.int32, (BASE, size), 0)
    picked = jnp.concatenate([jnp.where(lane == k, packed, 0.0) for k in range(BASE)], axis=0)
    group = same.astype(F32).astype(jnp.bfloat16)
    spread = None
    rest = picked
    for _ in range(3):
        part = rest.astype(jnp.bfloat16)
        rest = rest - part.astype(F32)
        term = jnp.dot(part, group, preferred_element_type=F32)
        spread = term if spread is None else spread + term
    state = jnp.where(sub == lane, 1.0, 0.0).astype(F32)
    for k in range(BASE):
        coupling = spread[k * BASE:(k + 1) * BASE]
        solved = state[k:k + 1] * (1.0 / coupling[k:k + 1])
        state = jnp.where(sub == k, solved, jnp.where(sub > k, state - coupling * solved, state))
    return jnp.where(same, jnp.concatenate([state] * count, axis=0), 0.0)


def grow_inverse(block, inverse, start, end):
    size = block.shape[0]
    row = lax.broadcasted_iota(jnp.int32, (size, size), 0)
    column = lax.broadcasted_iota(jnp.int32, (size, size), 1)
    width = start
    while width < end:
        above = ((row // width) + 1 == (column // width)) & ((row // (2 * width)) == (column // (2 * width)))
        parts = split(inverse)
        middle = product(parts, split(jnp.where(above, block, 0.0)))
        inverse = inverse - product(split(middle), parts)
        width *= 2
    return inverse


def pack(upper):
    size = upper.shape[0]
    rest = upper[:, TILE:]
    beside = jnp.concatenate([rest[:size // 2], rest[size // 2:]], axis=1)
    return jnp.concatenate([upper[:TILE, :TILE], beside], axis=0)


def unpack(packed, size):
    beside = packed[TILE:]
    rest = jnp.concatenate([beside[:, :size - TILE], beside[:, size - TILE:]], axis=0)
    first = jnp.concatenate([packed[:TILE], jnp.zeros((size - TILE, TILE), F32)], axis=0)
    return jnp.concatenate([first, rest], axis=1)


def kernel(sections, cands, archive, candidates, lengths, factor, whitened, covariance,
           both_archive, near, far, own_candidates, own_lengths, chosen, points, inverses,
           high_weights, low_weights, panels, peers, columns, turned, sums, pieces,
           load, far_load, in_send, in_recv, ch_send, ch_recv, y_send, y_recv, s_send, s_recv,
           pan_send, pan_recv, out_send, out_recv, pass_send, peer_recv, sum_send, sum_recv, ready):
    me = lax.axis_index("chain")
    c = lax.axis_index("cand")
    z, y = me // 2, me % 2
    steps = sections // 2
    core = c % 2
    height = factor.shape[0]
    pair = 2 * height
    cover = -(-height // 128) * 128
    width = candidates.shape[1]
    half = width // 2
    ratio = (2 * cands) // sections
    slab = half * ratio
    strip = height // 2
    partner = 2 * z + (1 - y)
    sibling = c + 1 - 2 * core
    mine = pl.ds(pl.multiple_of(core * strip, 8), strip)
    others = pl.ds(pl.multiple_of((1 - core) * strip, 8), strip)
    diagonal = pl.multiple_of(z * pair, 128)

    def remote(source, target, send, recv, where):
        return pltpu.make_async_remote_copy(
            src_ref=source, dst_ref=target, send_sem=send, recv_sem=recv, device_id=where, device_id_type=MESH)

    def far_copy(j):
        return pltpu.make_async_copy(factor.at[:, j * pair:(j + 1) * pair], far.at[j, y], far_load.at[j])

    near_copy = pltpu.make_async_copy(factor.at[:, pl.ds(diagonal, pair)], near.at[y], load.at[0])
    lengths_copy = pltpu.make_async_copy(lengths, own_lengths, load.at[1])
    candidates_copy = pltpu.make_async_copy(candidates, own_candidates, load.at[2])
    archive_copy = pltpu.make_async_copy(archive, both_archive.at[y], load.at[3])
    near_copy.start()
    lengths_copy.start()
    candidates_copy.start()
    archive_copy.start()

    barrier = pltpu.get_barrier_semaphore()
    pl.semaphore_signal(barrier, inc=1, device_id=(partner, c), device_id_type=MESH)

    @pl.when(z > 0)
    def _():
        pl.semaphore_signal(barrier, inc=1, device_id=(lax.rem(me + sections - 2, sections), c), device_id_type=MESH)

    @pl.when(z < steps - 1)
    def _():
        pl.semaphore_signal(barrier, inc=1, device_id=(lax.rem(me + 2, sections), c), device_id_type=MESH)
    for d in range(1, cands):
        pl.semaphore_signal(barrier, inc=1, device_id=(me, lax.rem(c + d, cands)), device_id_type=MESH)
    for j in range(steps - 1):
        @pl.when(z > j)
        def _(j=j):
            far_copy(j).start()

    near_copy.wait()
    strip_of_pair = near[y]
    block = jnp.where(y == 0, strip_of_pair[:, :height], strip_of_pair[:, height:])
    small = jnp.transpose(base_inverse(block))
    block = jnp.transpose(block)
    small = grow_inverse(block, small, BASE, 2 * BASE)
    lengths_copy.wait()
    candidates_copy.wait()
    archive_copy.wait()
    scale_row = 1.0 / own_lengths[...]
    scaling = jnp.transpose(jnp.broadcast_to(scale_row, (8, scale_row.shape[1])))[:, :1]
    owner_cand = (me * slab) // width

    neighbours = cands + jnp.where(z > 0, 1, 0) + jnp.where(z < steps - 1, 1, 0)
    pl.semaphore_wait(barrier, neighbours)

    send_in = remote(archive, both_archive.at[y], in_send, in_recv, (partner, c))
    send_in.start()

    def area(e, who, rows):
        if e == 1:
            return near.at[1, rows, pl.ds(0, cover)]
        return far.at[e - 2, who, rows]

    def across(e):
        if e == 0:
            return remote(inverses.at[y], inverses.at[y], y_send.at[e], y_recv.at[e], (partner, c))
        if e == 1:
            source = factor.at[mine, pl.ds(diagonal, cover)]
        else:
            source = factor.at[mine, pl.ds((e - 2) * pair, pair)]
        return remote(source, area(e, y, mine), y_send.at[e], y_recv.at[e], (partner, c))

    def across_recv(e):
        if e == 0:
            return remote(inverses.at[1 - y], inverses.at[1 - y], y_send.at[e], y_recv.at[e], (partner, c))
        return remote(area(e, 1 - y, mine), area(e, 1 - y, mine), y_send.at[e], y_recv.at[e], (partner, c))

    def beside(e):
        return remote(area(e, 1 - y, mine), area(e, 1 - y, mine), s_send.at[e], s_recv.at[e], (me, sibling))

    def beside_recv(e):
        return remote(area(e, 1 - y, others), area(e, 1 - y, others), s_send.at[e], s_recv.at[e], (me, sibling))

    @pl.when(y == 1)
    def _():
        across(1).start()
    early = min(2, steps - 1)
    for j in range(early):
        @pl.when(z > j)
        def _(j=j):
            across(j + 2).start()

    def chosen_copy(d):
        return remote(candidates, chosen, ch_send.at[d - 1], ch_recv, (me, lax.rem(c + d, cands)))

    @pl.when(c == owner_cand)
    def _():
        for d in range(1, cands):
            chosen_copy(d).start()
        chosen[...] = own_candidates[...]

    inverses[y] = pack(grow_inverse(block, small, 2 * BASE, height))
    across(0).start()
    for j in range(early, steps - 1):
        @pl.when(z > j)
        def _(j=j):
            across(j + 2).start()

    @pl.when(y == 0)
    def _():
        across_recv(1).wait_recv()
        beside(1).start()

    points[...] = jnp.transpose(own_candidates[...] * scaling)
    own_points = points[pl.ds(pl.multiple_of(y * half, 8), half), :]
    send_in.wait_send()
    remote(archive, both_archive.at[1 - y], in_send, in_recv, (partner, c)).wait_recv()
    cross = jnp.concatenate(
        [matern(own_points, both_archive[0] * scaling), matern(own_points, both_archive[1] * scaling)], axis=1)
    columns[y] = cross

    @pl.when(y == 0)
    def _():
        beside_recv(1).wait_recv()

    coupling = split(jnp.transpose(near[1][:, :height]))

    def pass_far(j):
        far_copy(j).wait()
        across_recv(j + 2).wait_recv()
        beside(j + 2).start()

    def turn_far(j):
        beside_recv(j + 2).wait_recv()
        high, low = split(jnp.transpose(far[j].reshape(pair, pair)))
        high_weights[j] = high
        low_weights[j] = low

    for j in range(early):
        @pl.when(z > j)
        def _(j=j):
            pass_far(j)
    for j in range(early):
        @pl.when(z > j)
        def _(j=j):
            turn_far(j)
    @pl.when((z > 0) & (z < steps - 1))
    def _():
        pl.semaphore_wait(ready, 1)

    @pl.when(z > 0)
    def _():
        pl.semaphore_signal(ready, inc=1, device_id=(lax.rem(me + sections - 2, sections), c), device_id_type=MESH)

    across_recv(0).wait_recv()
    upper_inverse = unpack(inverses[0], height)
    lower_inverse = unpack(inverses[1], height)
    upper = split(upper_inverse)
    lower = split(lower_inverse)
    between = split(product(coupling, lower))
    part = half // CHUNKS
    half_count = cands // 2

    def rows_of(k):
        return pl.ds(k * part, part)

    def launch(j, k):
        return remote(columns.at[y, rows_of(k)], panels.at[j, rows_of(k)], out_send.at[0, k], pan_recv.at[j, k],
                      (lax.rem(me + 2, sections), c))

    def to_peer(d, k):
        return remote(columns.at[y, rows_of(k)], peers.at[c, rows_of(k)], out_send.at[1 + d, k], peer_recv.at[c, k],
                      (me, lax.rem(c + 2 * d, cands)))

    def to_sibling(k):
        return remote(columns.at[y, rows_of(k)], peers.at[c, rows_of(k)], out_send.at[1, k], peer_recv.at[c, k],
                      (me, sibling))

    def to_partner(k):
        return remote(columns.at[y, rows_of(k)], columns.at[y, rows_of(k)], out_send.at[1 + half_count, k],
                      out_recv.at[k], (partner, c))

    def emit(j, k):
        if j < steps - 1:
            launch(j, k).start()
        for d in range(1, half_count):
            to_peer(d, k).start()
        to_partner(k).start()
        to_sibling(k).start()

    def solve(k):
        rows = slice(k * part, (k + 1) * part)
        residue = columns[y, rows]
        first = product(split(residue[:, :height]), upper)
        second = product(split(residue[:, height:]), lower) - product(split(first), between)
        columns[y, rows] = jnp.concatenate([first, second], axis=1)

    @pl.when(z == 0)
    def _():
        for k in range(CHUNKS):
            solve(k)
            emit(0, k)

    def onward(j, k):
        return remote(panels.at[j, rows_of(k)], panels.at[j, rows_of(k)], pan_send.at[j, k], pan_recv.at[j, k],
                      (lax.rem(me + 2, sections), c))

    def subtract(j, k, weights):
        onward(j, k).wait_recv()
        if j < steps - 2:
            @pl.when(z < steps - 1)
            def _():
                onward(j, k).start()
        rows = slice(k * part, (k + 1) * part)
        columns[y, rows] = columns[y, rows] - product(split(panels[j, rows]), weights)

    @pl.when(z > 0)
    def _():
        corner = -product(upper, between)
        whole = split(jnp.concatenate([
            jnp.concatenate([upper_inverse, corner], axis=1),
            jnp.concatenate([jnp.zeros((height, height), F32), lower_inverse], axis=1)], axis=0))
        for j in range(steps - 1):
            @pl.when(z > j)
            def _(j=j):
                if j >= early:
                    pass_far(j)
                    turn_far(j)
                high, low = split(product((high_weights[j], low_weights[j]), whole))
                high_weights[j] = high
                low_weights[j] = low
            if j == 0:
                columns[y] = product(split(columns[y]), whole)
        for j in range(steps - 1):
            @pl.when(z > j)
            def _(j=j):
                for k in range(CHUNKS):
                    subtract(j, k, (high_weights[j], low_weights[j]))

                    @pl.when(z == j + 1)
                    def _():
                        emit(j + 1, k)

    def from_peer(q, k):
        return remote(columns.at[y, rows_of(k)], peers.at[q, rows_of(k)], out_send.at[1, k], peer_recv.at[q, k],
                      (me, sibling))

    def pass_on(d, k):
        q = lax.rem(c + 2 * d, cands)
        return remote(peers.at[q, rows_of(k)], peers.at[q, rows_of(k)], pass_send.at[d, k], peer_recv.at[q, k],
                      (me, sibling))

    def wait_peer(q):
        for k in range(CHUNKS):
            from_peer(q, k).wait_recv()

    peers[c] = columns[y]

    @pl.when(c != owner_cand)
    def _():
        remote(candidates, chosen, ch_send.at[0], ch_recv, (me, sibling)).wait_recv()

    points[...] = jnp.transpose(chosen[...] * scaling)
    within = pl.multiple_of((me * slab) % width, 8)
    covariance[...] = matern(points[pl.ds(within, slab), :], own_candidates[...] * scaling)

    for k in range(CHUNKS):
        for d in range(1, half_count):
            from_peer(lax.rem(c + 2 * d, cands), k).wait_recv()
            pass_on(d, k).start()
    for k in range(CHUNKS):
        remote(columns.at[y, rows_of(k)], columns.at[1 - y, rows_of(k)], out_send.at[1, k], out_recv.at[k],
               (partner, c)).wait_recv()
    turned[...] = jnp.transpose(columns[...].reshape(width, pair))
    facing = split(turned[...])

    def piece_copy(q):
        group = 2 * q + y
        return remote(pieces.at[q], sums.at[z, group % ratio], sum_send.at[q],
                      sum_recv.at[z, group % ratio], (group // ratio, c))

    def piece(q):
        group = 2 * q + y
        pieces[q] = product(split(peers[q]), facing)

        @pl.when(group // ratio != me)
        def _():
            piece_copy(q).start()

        @pl.when(group // ratio == me)
        def _():
            sums[z, group % ratio] = pieces[q]

    @pl.when(z == 0)
    def _():
        pl.semaphore_wait(ready, 1)

    piece(c)
    wait_peer(sibling)
    piece(sibling)
    for d in range(1, half_count):
        piece(lax.rem(c + 2 * d, cands))
    for d in range(1, half_count):
        q = lax.rem(sibling + 2 * d, cands)
        wait_peer(q)
        piece(q)

    whitened[...] = turned[pl.ds(pl.multiple_of(y * height, 8), height), :]

    for k in range(ratio):
        for step in range(steps):
            sender = 2 * step + lax.rem(ratio * me + k, 2)

            @pl.when(sender != me)
            def _(k=k, step=step):
                remote(pieces.at[0], sums.at[step, k], sum_send.at[0], sum_recv.at[step, k], (partner, c)).wait_recv()
        total = functools.reduce(jnp.add, [sums[step, k] for step in range(steps)])
        covariance[k * half:(k + 1) * half] = covariance[k * half:(k + 1) * half] - total

    @pl.when(c == owner_cand)
    def _():
        for d in range(1, cands):
            chosen_copy(d).wait_send()
    across(0).wait_send()

    @pl.when(y == 1)
    def _():
        across(1).wait_send()

    @pl.when(y == 0)
    def _():
        beside(1).wait_send()
    for j in range(steps - 1):
        @pl.when(z > j)
        def _(j=j):
            across(j + 2).wait_send()
            beside(j + 2).wait_send()
            if j < steps - 2:
                @pl.when(z < steps - 1)
                def _():
                    for k in range(CHUNKS):
                        onward(j, k).wait_send()

        @pl.when(z == j)
        def _(j=j):
            for k in range(CHUNKS):
                launch(j, k).wait_send()
    for k in range(CHUNKS):
        for d in range(1, half_count):
            to_peer(d, k).wait_send()
            pass_on(d, k).wait_send()
        to_sibling(k).wait_send()
        to_partner(k).wait_send()
    for q in range(cands):
        @pl.when((2 * q + y) // ratio != me)
        def _(q=q):
            piece_copy(q).wait_send()


def shards(sections, cands, archive, candidates, lengths, factor):
    dims, height = archive.shape
    width = candidates.shape[1]
    pair, half, steps = 2 * height, width // 2, sections // 2
    ratio = (2 * cands) // sections
    vmem = pl.BlockSpec(memory_space=pltpu.VMEM)
    hbm = pl.BlockSpec(memory_space=pltpu.HBM)
    dma = pltpu.SemaphoreType.DMA
    return pl.pallas_call(
        functools.partial(kernel, sections, cands),
        out_shape=(jax.ShapeDtypeStruct((height, width), F32), jax.ShapeDtypeStruct((half * ratio, width), F32)),
        in_specs=[hbm] * 4,
        out_specs=(vmem, vmem),
        scratch_shapes=[
            pltpu.VMEM((2, dims, height), F32),
            pltpu.VMEM((2, height, pair), F32),
            pltpu.VMEM((steps - 1, 2, height, pair), F32),
            pltpu.VMEM((dims, width), F32),
            pltpu.VMEM((1, dims), F32),
            pltpu.VMEM((dims, width), F32),
            pltpu.VMEM((width, dims), F32),
            pltpu.VMEM((2, TILE + height // 2, TILE), F32),
            pltpu.VMEM((steps - 1, pair, pair), jnp.bfloat16),
            pltpu.VMEM((steps - 1, pair, pair), jnp.bfloat16),
            pltpu.VMEM((steps - 1, half, pair), F32),
            pltpu.VMEM((cands, half, pair), F32),
            pltpu.VMEM((2, half, pair), F32),
            pltpu.VMEM((pair, width), F32),
            pltpu.VMEM((steps, ratio, half, width), F32),
            pltpu.VMEM((cands, half, width), F32),
            dma((4,)), dma((steps - 1,)),
            dma, dma,
            dma((cands - 1,)), dma,
            dma((steps + 1,)), dma((steps + 1,)), dma((steps + 1,)), dma((steps + 1,)),
            dma((steps - 1, CHUNKS)), dma((steps - 1, CHUNKS)),
            dma((2 + cands // 2, CHUNKS)), dma((CHUNKS,)),
            dma((cands // 2, CHUNKS)), dma((cands, CHUNKS)),
            dma((cands,)), dma((steps, ratio)),
            pltpu.SemaphoreType.REGULAR,
        ],
        compiler_params=pltpu.CompilerParams(
            collective_id=0, has_side_effects=True, vmem_limit_bytes=48 * 1024 * 1024),
    )(*(pltpu.with_memory_space_constraint(x, pltpu.HBM)
        for x in (archive, candidates, lengths.reshape(1, dims), factor)))


def solution(mesh):
    return jax.shard_map(
        functools.partial(shards, mesh.shape["chain"], mesh.shape["cand"]),
        mesh=mesh,
        in_specs=(P(None, "chain"), P(None, "cand"), P(), P("chain", None)),
        out_specs=(P("chain", "cand"), P("chain", "cand")),
        check_vma=False,
    )
```

```python
import functools
import jax
import jax.numpy as jnp
from jax import lax
from jax.experimental import pallas as pl
from jax.experimental.pallas import tpu as pltpu
from jax.sharding import PartitionSpec as P

MESH = pl.DeviceIdType.MESH
F32 = jnp.float32
BASE = 32
TILE = 128
CHUNKS = 2


def split(value):
    high = value.astype(jnp.bfloat16)
    return high, (value - high.astype(F32)).astype(jnp.bfloat16)


def product(first, second, transposed=False):
    dims = (((1,), (1 if transposed else 0,)), ((), ()))
    dot = functools.partial(lax.dot_general, dimension_numbers=dims, preferred_element_type=F32)
    count = first[0].shape[0]
    stacked = dot(jnp.concatenate([first[0], first[1]], axis=0), second[0])
    return stacked[:count] + (stacked[count:] + dot(first[0], second[1]))


def matern(rows, columns):
    total = None
    for d in range(columns.shape[0]):
        differ = rows[:, d:d + 1] - columns[d:d + 1, :]
        total = differ * differ if total is None else total + differ * differ
    radius = jnp.sqrt(5.0 * total)
    return (1.0 + radius + radius * radius / 3.0) * jnp.exp(-radius)


def base_inverse(block):
    size = block.shape[0]
    count = size // BASE
    row = lax.broadcasted_iota(jnp.int32, (size, size), 0)
    column = lax.broadcasted_iota(jnp.int32, (size, size), 1)
    same = (row // BASE) == (column // BASE)
    kept = jnp.where(same, block, 0.0)
    packed = functools.reduce(jnp.add, [kept[b * BASE:(b + 1) * BASE] for b in range(count)])
    lane = lax.broadcasted_iota(jnp.int32, (BASE, size), 1) % BASE
    sub = lax.broadcasted_iota(jnp.int32, (BASE, size), 0)
    picked = jnp.concatenate([jnp.where(lane == k, packed, 0.0) for k in range(BASE)], axis=0)
    group = same.astype(F32).astype(jnp.bfloat16)
    spread = None
    rest = picked
    for _ in range(3):
        part = rest.astype(jnp.bfloat16)
        rest = rest - part.astype(F32)
        term = jnp.dot(part, group, preferred_element_type=F32)
        spread = term if spread is None else spread + term
    state = jnp.where(sub == lane, 1.0, 0.0).astype(F32)
    for k in range(BASE):
        coupling = spread[k * BASE:(k + 1) * BASE]
        solved = state[k:k + 1] * (1.0 / coupling[k:k + 1])
        state = jnp.where(sub == k, solved, jnp.where(sub > k, state - coupling * solved, state))
    return jnp.where(same, jnp.concatenate([state] * count, axis=0), 0.0)


def grow_inverse(block, inverse, start, end):
    size = block.shape[0]
    row = lax.broadcasted_iota(jnp.int32, (size, size), 0)
    column = lax.broadcasted_iota(jnp.int32, (size, size), 1)
    width = start
    while width < end:
        above = ((row // width) + 1 == (column // width)) & ((row // (2 * width)) == (column // (2 * width)))
        parts = split(inverse)
        middle = product(parts, split(jnp.where(above, block, 0.0)))
        inverse = inverse - product(split(middle), parts)
        width *= 2
    return inverse


def pack(upper):
    size = upper.shape[0]
    rest = upper[:, TILE:]
    beside = jnp.concatenate([rest[:size // 2], rest[size // 2:]], axis=1)
    return jnp.concatenate([upper[:TILE, :TILE], beside], axis=0)


def unpack(packed, size):
    beside = packed[TILE:]
    rest = jnp.concatenate([beside[:, :size - TILE], beside[:, size - TILE:]], axis=0)
    first = jnp.concatenate([packed[:TILE], jnp.zeros((size - TILE, TILE), F32)], axis=0)
    return jnp.concatenate([first, rest], axis=1)


def kernel(sections, cands, archive, candidates, lengths, factor, whitened, covariance,
           both_archive, near, far, own_candidates, own_lengths, chosen, points, inverses,
           high_weights, low_weights, panels, peers, columns, turned, sums, pieces,
           load, far_load, in_send, in_recv, ch_send, ch_recv, y_send, y_recv, s_send, s_recv,
           pan_send, pan_recv, out_send, out_recv, pass_send, peer_recv, sum_send, sum_recv, ready):
    me = lax.axis_index("chain")
    c = lax.axis_index("cand")
    z, y = me // 2, me % 2
    steps = sections // 2
    core = c % 2
    height = factor.shape[0]
    pair = 2 * height
    cover = -(-height // 128) * 128
    width = candidates.shape[1]
    half = width // 2
    ratio = (2 * cands) // sections
    slab = half * ratio
    strip = height // 2
    partner = 2 * z + (1 - y)
    sibling = c + 1 - 2 * core
    mine = pl.ds(pl.multiple_of(core * strip, 8), strip)
    others = pl.ds(pl.multiple_of((1 - core) * strip, 8), strip)
    diagonal = pl.multiple_of(z * pair, 128)

    def remote(source, target, send, recv, where):
        return pltpu.make_async_remote_copy(
            src_ref=source, dst_ref=target, send_sem=send, recv_sem=recv, device_id=where, device_id_type=MESH)

    def far_copy(j):
        return pltpu.make_async_copy(factor.at[:, j * pair:(j + 1) * pair], far.at[j, y], far_load.at[j])

    near_copy = pltpu.make_async_copy(factor.at[:, pl.ds(diagonal, pair)], near.at[y], load.at[0])
    lengths_copy = pltpu.make_async_copy(lengths, own_lengths, load.at[1])
    candidates_copy = pltpu.make_async_copy(candidates, own_candidates, load.at[2])
    archive_copy = pltpu.make_async_copy(archive, both_archive.at[y], load.at[3])
    near_copy.start()
    lengths_copy.start()
    candidates_copy.start()
    archive_copy.start()

    barrier = pltpu.get_barrier_semaphore()
    pl.semaphore_signal(barrier, inc=1, device_id=(partner, c), device_id_type=MESH)

    @pl.when(z > 0)
    def _():
        pl.semaphore_signal(barrier, inc=1, device_id=(lax.rem(me + sections - 2, sections), c), device_id_type=MESH)

    @pl.when(z < steps - 1)
    def _():
        pl.semaphore_signal(barrier, inc=1, device_id=(lax.rem(me + 2, sections), c), device_id_type=MESH)
    for d in range(1, cands):
        pl.semaphore_signal(barrier, inc=1, device_id=(me, lax.rem(c + d, cands)), device_id_type=MESH)
    for j in range(steps - 1):
        @pl.when(z > j)
        def _(j=j):
            far_copy(j).start()

    near_copy.wait()
    strip_of_pair = near[y]
    block = jnp.where(y == 0, strip_of_pair[:, :height], strip_of_pair[:, height:])
    small = jnp.transpose(base_inverse(block))
    block = jnp.transpose(block)
    small = grow_inverse(block, small, BASE, 2 * BASE)
    lengths_copy.wait()
    candidates_copy.wait()
    archive_copy.wait()
    scale_row = 1.0 / own_lengths[...]
    scaling = jnp.transpose(jnp.broadcast_to(scale_row, (8, scale_row.shape[1])))[:, :1]
    owner_cand = (me * slab) // width

    neighbours = cands + jnp.where(z > 0, 1, 0) + jnp.where(z < steps - 1, 1, 0)
    pl.semaphore_wait(barrier, neighbours)

    def announce():
        pl.semaphore_signal(ready, inc=1, device_id=(lax.rem(me + sections - 2, sections), c), device_id_type=MESH)

    @pl.when(z == steps - 1)
    def _():
        announce()

    send_in = remote(archive, both_archive.at[y], in_send, in_recv, (partner, c))
    send_in.start()

    def area(e, who, rows):
        if e == 1:
            return near.at[1, rows, pl.ds(0, cover)]
        return far.at[e - 2, who, rows]

    def across(e):
        if e == 0:
            return remote(inverses.at[y], inverses.at[y], y_send.at[e], y_recv.at[e], (partner, c))
        if e == 1:
            source = factor.at[mine, pl.ds(diagonal, cover)]
        else:
            source = factor.at[mine, pl.ds((e - 2) * pair, pair)]
        return remote(source, area(e, y, mine), y_send.at[e], y_recv.at[e], (partner, c))

    def across_recv(e):
        if e == 0:
            return remote(inverses.at[1 - y], inverses.at[1 - y], y_send.at[e], y_recv.at[e], (partner, c))
        return remote(area(e, 1 - y, mine), area(e, 1 - y, mine), y_send.at[e], y_recv.at[e], (partner, c))

    def beside(e):
        return remote(area(e, 1 - y, mine), area(e, 1 - y, mine), s_send.at[e], s_recv.at[e], (me, sibling))

    def beside_recv(e):
        return remote(area(e, 1 - y, others), area(e, 1 - y, others), s_send.at[e], s_recv.at[e], (me, sibling))

    @pl.when(y == 1)
    def _():
        across(1).start()
    early = min(2, steps - 1)
    for j in range(early):
        @pl.when(z > j)
        def _(j=j):
            across(j + 2).start()

    def chosen_copy(d):
        return remote(candidates, chosen, ch_send.at[d - 1], ch_recv, (me, lax.rem(c + d, cands)))

    @pl.when(c == owner_cand)
    def _():
        for d in range(1, cands):
            chosen_copy(d).start()
        chosen[...] = own_candidates[...]

    inverses[y] = pack(grow_inverse(block, small, 2 * BASE, height))
    across(0).start()
    for j in range(early, steps - 1):
        @pl.when(z > j)
        def _(j=j):
            across(j + 2).start()

    @pl.when(y == 0)
    def _():
        across_recv(1).wait_recv()
        beside(1).start()

    points[...] = jnp.transpose(own_candidates[...] * scaling)
    own_points = points[pl.ds(pl.multiple_of(y * half, 8), half), :]
    send_in.wait_send()
    remote(archive, both_archive.at[1 - y], in_send, in_recv, (partner, c)).wait_recv()
    cross = jnp.concatenate(
        [matern(own_points, both_archive[0] * scaling), matern(own_points, both_archive[1] * scaling)], axis=1)
    columns[y] = cross

    @pl.when(y == 0)
    def _():
        beside_recv(1).wait_recv()

    coupling = split(jnp.transpose(near[1][:, :height]))

    def pass_far(j):
        far_copy(j).wait()
        across_recv(j + 2).wait_recv()
        beside(j + 2).start()

    def turn_far(j):
        beside_recv(j + 2).wait_recv()
        high, low = split(jnp.transpose(far[j].reshape(pair, pair)))
        high_weights[j] = high
        low_weights[j] = low

    for j in range(early):
        @pl.when(z > j)
        def _(j=j):
            pass_far(j)
    for j in range(early):
        @pl.when(z > j)
        def _(j=j):
            turn_far(j)
    across_recv(0).wait_recv()
    upper_inverse = unpack(inverses[0], height)
    lower_inverse = unpack(inverses[1], height)
    upper = split(upper_inverse)
    lower = split(lower_inverse)
    between = split(product(coupling, lower))
    part = half // CHUNKS
    half_count = cands // 2

    def rows_of(k):
        return pl.ds(k * part, part)

    def launch(j, k):
        return remote(columns.at[y, rows_of(k)], panels.at[j, rows_of(k)], out_send.at[0, k], pan_recv.at[j, k],
                      (lax.rem(me + 2, sections), c))

    def to_peer(d, k):
        return remote(columns.at[y, rows_of(k)], peers.at[c, rows_of(k)], out_send.at[1 + d, k], peer_recv.at[c, k],
                      (me, lax.rem(c + 2 * d, cands)))

    def to_sibling(k):
        return remote(columns.at[y, rows_of(k)], peers.at[c, rows_of(k)], out_send.at[1, k], peer_recv.at[c, k],
                      (me, sibling))

    def to_partner(k):
        return remote(columns.at[y, rows_of(k)], columns.at[y, rows_of(k)], out_send.at[1 + half_count, k],
                      out_recv.at[k], (partner, c))

    def emit(j, k):
        if j < steps - 1:
            launch(j, k).start()
        for d in range(1, half_count):
            to_peer(d, k).start()
        to_partner(k).start()
        to_sibling(k).start()

    def solve(k):
        rows = slice(k * part, (k + 1) * part)
        residue = columns[y, rows]
        first = product(split(residue[:, :height]), upper)
        second = product(split(residue[:, height:]), lower) - product(split(first), between)
        columns[y, rows] = jnp.concatenate([first, second], axis=1)

    @pl.when(z == 0)
    def _():
        for k in range(CHUNKS):
            solve(k)
            emit(0, k)

    def onward(j, k):
        return remote(panels.at[j, rows_of(k)], panels.at[j, rows_of(k)], pan_send.at[j, k], pan_recv.at[j, k],
                      (lax.rem(me + 2, sections), c))

    def subtract(j, k, weights):
        onward(j, k).wait_recv()
        if j < steps - 2:
            @pl.when(z < steps - 1)
            def _():
                onward(j, k).start()
        rows = slice(k * part, (k + 1) * part)
        columns[y, rows] = columns[y, rows] - product(split(panels[j, rows]), weights)

    @pl.when(z > 0)
    def _():
        corner = -product(upper, between)
        whole = split(jnp.concatenate([
            jnp.concatenate([upper_inverse, corner], axis=1),
            jnp.concatenate([jnp.zeros((height, height), F32), lower_inverse], axis=1)], axis=0))
        for j in range(steps - 1):
            @pl.when(z > j)
            def _(j=j):
                if j >= early:
                    pass_far(j)
                    turn_far(j)
                high, low = split(product((high_weights[j], low_weights[j]), whole))
                high_weights[j] = high
                low_weights[j] = low
            if j == 0:
                columns[y] = product(split(columns[y]), whole)
        for j in range(steps - 1):
            @pl.when(z > j)
            def _(j=j):
                for k in range(CHUNKS):
                    subtract(j, k, (high_weights[j], low_weights[j]))

                    @pl.when(z == j + 1)
                    def _():
                        emit(j + 1, k)

    def from_peer(q, k):
        return remote(columns.at[y, rows_of(k)], peers.at[q, rows_of(k)], out_send.at[1, k], peer_recv.at[q, k],
                      (me, sibling))

    def pass_on(d, k):
        q = lax.rem(c + 2 * d, cands)
        return remote(peers.at[q, rows_of(k)], peers.at[q, rows_of(k)], pass_send.at[d, k], peer_recv.at[q, k],
                      (me, sibling))

    def wait_peer(q):
        for k in range(CHUNKS):
            from_peer(q, k).wait_recv()

    peers[c] = columns[y]

    @pl.when(c != owner_cand)
    def _():
        remote(candidates, chosen, ch_send.at[0], ch_recv, (me, sibling)).wait_recv()

    points[...] = jnp.transpose(chosen[...] * scaling)
    within = pl.multiple_of((me * slab) % width, 8)
    covariance[...] = matern(points[pl.ds(within, slab), :], own_candidates[...] * scaling)

    for k in range(CHUNKS):
        for d in range(1, half_count):
            from_peer(lax.rem(c + 2 * d, cands), k).wait_recv()
            pass_on(d, k).start()
    for k in range(CHUNKS):
        remote(columns.at[y, rows_of(k)], columns.at[1 - y, rows_of(k)], out_send.at[1, k], out_recv.at[k],
               (partner, c)).wait_recv()
    turned[...] = jnp.transpose(columns[...].reshape(width, pair))
    facing = split(turned[...])

    def piece_copy(q):
        group = 2 * q + y
        return remote(pieces.at[q], sums.at[z, group % ratio], sum_send.at[q],
                      sum_recv.at[z, group % ratio], (group // ratio, c))

    def piece(q):
        group = 2 * q + y
        pieces[q] = product(split(peers[q]), facing)

        @pl.when(group // ratio != me)
        def _():
            piece_copy(q).start()

        @pl.when(group // ratio == me)
        def _():
            sums[z, group % ratio] = pieces[q]

    @pl.when(z < steps - 1)
    def _():
        pl.semaphore_wait(ready, 1)

    @pl.when((z > 0) & (z < steps - 1))
    def _():
        announce()

    piece(c)
    wait_peer(sibling)
    piece(sibling)
    for d in range(1, half_count):
        piece(lax.rem(c + 2 * d, cands))
    for d in range(1, half_count):
        q = lax.rem(sibling + 2 * d, cands)
        wait_peer(q)
        piece(q)

    whitened[...] = turned[pl.ds(pl.multiple_of(y * height, 8), height), :]

    for k in range(ratio):
        for step in range(steps):
            sender = 2 * step + lax.rem(ratio * me + k, 2)

            @pl.when(sender != me)
            def _(k=k, step=step):
                remote(pieces.at[0], sums.at[step, k], sum_send.at[0], sum_recv.at[step, k], (partner, c)).wait_recv()
        total = functools.reduce(jnp.add, [sums[step, k] for step in range(steps)])
        covariance[k * half:(k + 1) * half] = covariance[k * half:(k + 1) * half] - total

    @pl.when(c == owner_cand)
    def _():
        for d in range(1, cands):
            chosen_copy(d).wait_send()
    across(0).wait_send()

    @pl.when(y == 1)
    def _():
        across(1).wait_send()

    @pl.when(y == 0)
    def _():
        beside(1).wait_send()
    for j in range(steps - 1):
        @pl.when(z > j)
        def _(j=j):
            across(j + 2).wait_send()
            beside(j + 2).wait_send()
            if j < steps - 2:
                @pl.when(z < steps - 1)
                def _():
                    for k in range(CHUNKS):
                        onward(j, k).wait_send()

        @pl.when(z == j)
        def _(j=j):
            for k in range(CHUNKS):
                launch(j, k).wait_send()
    for k in range(CHUNKS):
        for d in range(1, half_count):
            to_peer(d, k).wait_send()
            pass_on(d, k).wait_send()
        to_sibling(k).wait_send()
        to_partner(k).wait_send()
    for q in range(cands):
        @pl.when((2 * q + y) // ratio != me)
        def _(q=q):
            piece_copy(q).wait_send()


def shards(sections, cands, archive, candidates, lengths, factor):
    dims, height = archive.shape
    width = candidates.shape[1]
    pair, half, steps = 2 * height, width // 2, sections // 2
    ratio = (2 * cands) // sections
    vmem = pl.BlockSpec(memory_space=pltpu.VMEM)
    hbm = pl.BlockSpec(memory_space=pltpu.HBM)
    dma = pltpu.SemaphoreType.DMA
    return pl.pallas_call(
        functools.partial(kernel, sections, cands),
        out_shape=(jax.ShapeDtypeStruct((height, width), F32), jax.ShapeDtypeStruct((half * ratio, width), F32)),
        in_specs=[hbm] * 4,
        out_specs=(vmem, vmem),
        scratch_shapes=[
            pltpu.VMEM((2, dims, height), F32),
            pltpu.VMEM((2, height, pair), F32),
            pltpu.VMEM((steps - 1, 2, height, pair), F32),
            pltpu.VMEM((dims, width), F32),
            pltpu.VMEM((1, dims), F32),
            pltpu.VMEM((dims, width), F32),
            pltpu.VMEM((width, dims), F32),
            pltpu.VMEM((2, TILE + height // 2, TILE), F32),
            pltpu.VMEM((steps - 1, pair, pair), jnp.bfloat16),
            pltpu.VMEM((steps - 1, pair, pair), jnp.bfloat16),
            pltpu.VMEM((steps - 1, half, pair), F32),
            pltpu.VMEM((cands, half, pair), F32),
            pltpu.VMEM((2, half, pair), F32),
            pltpu.VMEM((pair, width), F32),
            pltpu.VMEM((steps, ratio, half, width), F32),
            pltpu.VMEM((cands, half, width), F32),
            dma((4,)), dma((steps - 1,)),
            dma, dma,
            dma((cands - 1,)), dma,
            dma((steps + 1,)), dma((steps + 1,)), dma((steps + 1,)), dma((steps + 1,)),
            dma((steps - 1, CHUNKS)), dma((steps - 1, CHUNKS)),
            dma((2 + cands // 2, CHUNKS)), dma((CHUNKS,)),
            dma((cands // 2, CHUNKS)), dma((cands, CHUNKS)),
            dma((cands,)), dma((steps, ratio)),
            pltpu.SemaphoreType.REGULAR,
        ],
        compiler_params=pltpu.CompilerParams(
            collective_id=0, has_side_effects=True, vmem_limit_bytes=48 * 1024 * 1024),
    )(*(pltpu.with_memory_space_constraint(x, pltpu.HBM)
        for x in (archive, candidates, lengths.reshape(1, dims), factor)))


def solution(mesh):
    return jax.shard_map(
        functools.partial(shards, mesh.shape["chain"], mesh.shape["cand"]),
        mesh=mesh,
        in_specs=(P(None, "chain"), P(None, "cand"), P(), P("chain", None)),
        out_specs=(P("chain", "cand"), P("chain", "cand")),
        check_vma=False,
    )
```

```python
import functools
import jax
import jax.numpy as jnp
from jax import lax
from jax.experimental import pallas as pl
from jax.experimental.pallas import tpu as pltpu
from jax.sharding import PartitionSpec as P

MESH = pl.DeviceIdType.MESH
F32 = jnp.float32
BASE = 32
TILE = 128
CHUNKS = 2


def split(value):
    high = value.astype(jnp.bfloat16)
    return high, (value - high.astype(F32)).astype(jnp.bfloat16)


def product(first, second, transposed=False):
    dims = (((1,), (1 if transposed else 0,)), ((), ()))
    dot = functools.partial(lax.dot_general, dimension_numbers=dims, preferred_element_type=F32)
    count = first[0].shape[0]
    stacked = dot(jnp.concatenate([first[0], first[1]], axis=0), second[0])
    return stacked[:count] + (stacked[count:] + dot(first[0], second[1]))


def matern(rows, columns):
    total = None
    for d in range(columns.shape[0]):
        differ = rows[:, d:d + 1] - columns[d:d + 1, :]
        total = differ * differ if total is None else total + differ * differ
    radius = jnp.sqrt(5.0 * total)
    return (1.0 + radius + radius * radius / 3.0) * jnp.exp(-radius)


def base_inverse(block):
    size = block.shape[0]
    count = size // BASE
    row = lax.broadcasted_iota(jnp.int32, (size, size), 0)
    column = lax.broadcasted_iota(jnp.int32, (size, size), 1)
    same = (row // BASE) == (column // BASE)
    kept = jnp.where(same, block, 0.0)
    packed = functools.reduce(jnp.add, [kept[b * BASE:(b + 1) * BASE] for b in range(count)])
    lane = lax.broadcasted_iota(jnp.int32, (BASE, size), 1) % BASE
    sub = lax.broadcasted_iota(jnp.int32, (BASE, size), 0)
    picked = jnp.concatenate([jnp.where(lane == k, packed, 0.0) for k in range(BASE)], axis=0)
    group = same.astype(F32).astype(jnp.bfloat16)
    spread = None
    rest = picked
    for _ in range(3):
        part = rest.astype(jnp.bfloat16)
        rest = rest - part.astype(F32)
        term = jnp.dot(part, group, preferred_element_type=F32)
        spread = term if spread is None else spread + term
    state = jnp.where(sub == lane, 1.0, 0.0).astype(F32)
    for k in range(BASE):
        coupling = spread[k * BASE:(k + 1) * BASE]
        solved = state[k:k + 1] * (1.0 / coupling[k:k + 1])
        state = jnp.where(sub == k, solved, jnp.where(sub > k, state - coupling * solved, state))
    return jnp.where(same, jnp.concatenate([state] * count, axis=0), 0.0)


def grow_inverse(block, inverse, start, end):
    size = block.shape[0]
    row = lax.broadcasted_iota(jnp.int32, (size, size), 0)
    column = lax.broadcasted_iota(jnp.int32, (size, size), 1)
    width = start
    while width < end:
        above = ((row // width) + 1 == (column // width)) & ((row // (2 * width)) == (column // (2 * width)))
        parts = split(inverse)
        middle = product(parts, split(jnp.where(above, block, 0.0)))
        inverse = inverse - product(split(middle), parts)
        width *= 2
    return inverse


def pack(upper):
    size = upper.shape[0]
    rest = upper[:, TILE:]
    beside = jnp.concatenate([rest[:size // 2], rest[size // 2:]], axis=1)
    return jnp.concatenate([upper[:TILE, :TILE], beside], axis=0)


def unpack(packed, size):
    beside = packed[TILE:]
    rest = jnp.concatenate([beside[:, :size - TILE], beside[:, size - TILE:]], axis=0)
    first = jnp.concatenate([packed[:TILE], jnp.zeros((size - TILE, TILE), F32)], axis=0)
    return jnp.concatenate([first, rest], axis=1)


def kernel(sections, cands, archive, candidates, lengths, factor, whitened, covariance,
           both_archive, near, far, own_candidates, own_lengths, chosen, points, inverses,
           high_weights, low_weights, panels, peers, columns, turned, sums, pieces,
           load, far_load, in_send, in_recv, ch_send, ch_recv, y_send, y_recv, s_send, s_recv,
           pan_send, pan_recv, out_send, out_recv, pass_send, peer_recv, sum_send, sum_recv, ready):
    me = lax.axis_index("chain")
    c = lax.axis_index("cand")
    z, y = me // 2, me % 2
    steps = sections // 2
    core = c % 2
    height = factor.shape[0]
    pair = 2 * height
    cover = -(-height // 128) * 128
    width = candidates.shape[1]
    half = width // 2
    ratio = (2 * cands) // sections
    slab = half * ratio
    strip = height // 2
    partner = 2 * z + (1 - y)
    sibling = c + 1 - 2 * core
    mine = pl.ds(pl.multiple_of(core * strip, 8), strip)
    others = pl.ds(pl.multiple_of((1 - core) * strip, 8), strip)
    diagonal = pl.multiple_of(z * pair, 128)

    def remote(source, target, send, recv, where):
        return pltpu.make_async_remote_copy(
            src_ref=source, dst_ref=target, send_sem=send, recv_sem=recv, device_id=where, device_id_type=MESH)

    def far_copy(j):
        return pltpu.make_async_copy(factor.at[:, j * pair:(j + 1) * pair], far.at[j, y], far_load.at[j])

    near_copy = pltpu.make_async_copy(factor.at[:, pl.ds(diagonal, pair)], near.at[y], load.at[0])
    lengths_copy = pltpu.make_async_copy(lengths, own_lengths, load.at[1])
    candidates_copy = pltpu.make_async_copy(candidates, own_candidates, load.at[2])
    archive_copy = pltpu.make_async_copy(archive, both_archive.at[y], load.at[3])
    near_copy.start()
    lengths_copy.start()
    candidates_copy.start()
    archive_copy.start()

    barrier = pltpu.get_barrier_semaphore()
    pl.semaphore_signal(barrier, inc=1, device_id=(partner, c), device_id_type=MESH)

    @pl.when(z > 0)
    def _():
        pl.semaphore_signal(barrier, inc=1, device_id=(lax.rem(me + sections - 2, sections), c), device_id_type=MESH)

    @pl.when(z < steps - 1)
    def _():
        pl.semaphore_signal(barrier, inc=1, device_id=(lax.rem(me + 2, sections), c), device_id_type=MESH)
    for d in range(1, cands):
        pl.semaphore_signal(barrier, inc=1, device_id=(me, lax.rem(c + d, cands)), device_id_type=MESH)
    for j in range(steps - 1):
        @pl.when(z > j)
        def _(j=j):
            far_copy(j).start()

    near_copy.wait()
    strip_of_pair = near[y]
    block = jnp.where(y == 0, strip_of_pair[:, :height], strip_of_pair[:, height:])
    small = jnp.transpose(base_inverse(block))
    block = jnp.transpose(block)
    small = grow_inverse(block, small, BASE, 4 * BASE)
    lengths_copy.wait()
    candidates_copy.wait()
    archive_copy.wait()
    scale_row = 1.0 / own_lengths[...]
    scaling = jnp.transpose(jnp.broadcast_to(scale_row, (8, scale_row.shape[1])))[:, :1]
    owner_cand = (me * slab) // width

    neighbours = cands + jnp.where(z > 0, 1, 0) + jnp.where(z < steps - 1, 1, 0)
    pl.semaphore_wait(barrier, neighbours)

    def announce():
        pl.semaphore_signal(ready, inc=1, device_id=(lax.rem(me + sections - 2, sections), c), device_id_type=MESH)

    @pl.when(z == steps - 1)
    def _():
        announce()

    send_in = remote(archive, both_archive.at[y], in_send, in_recv, (partner, c))
    send_in.start()

    def area(e, who, rows):
        if e == 1:
            return near.at[1, rows, pl.ds(0, cover)]
        return far.at[e - 2, who, rows]

    def across(e):
        if e == 0:
            return remote(inverses.at[y], inverses.at[y], y_send.at[e], y_recv.at[e], (partner, c))
        if e == 1:
            source = factor.at[mine, pl.ds(diagonal, cover)]
        else:
            source = factor.at[mine, pl.ds((e - 2) * pair, pair)]
        return remote(source, area(e, y, mine), y_send.at[e], y_recv.at[e], (partner, c))

    def across_recv(e):
        if e == 0:
            return remote(inverses.at[1 - y], inverses.at[1 - y], y_send.at[e], y_recv.at[e], (partner, c))
        return remote(area(e, 1 - y, mine), area(e, 1 - y, mine), y_send.at[e], y_recv.at[e], (partner, c))

    def beside(e):
        return remote(area(e, 1 - y, mine), area(e, 1 - y, mine), s_send.at[e], s_recv.at[e], (me, sibling))

    def beside_recv(e):
        return remote(area(e, 1 - y, others), area(e, 1 - y, others), s_send.at[e], s_recv.at[e], (me, sibling))

    @pl.when(y == 1)
    def _():
        across(1).start()
    early = min(2, steps - 1)
    for j in range(early):
        @pl.when(z > j)
        def _(j=j):
            across(j + 2).start()

    def chosen_copy(d):
        return remote(candidates, chosen, ch_send.at[d - 1], ch_recv, (me, lax.rem(c + d, cands)))

    @pl.when(c == owner_cand)
    def _():
        for d in range(1, cands):
            chosen_copy(d).start()
        chosen[...] = own_candidates[...]

    inverses[y] = pack(grow_inverse(block, small, 4 * BASE, height))
    across(0).start()
    for j in range(early, steps - 1):
        @pl.when(z > j)
        def _(j=j):
            across(j + 2).start()

    @pl.when(y == 0)
    def _():
        across_recv(1).wait_recv()
        beside(1).start()

    points[...] = jnp.transpose(own_candidates[...] * scaling)
    own_points = points[pl.ds(pl.multiple_of(y * half, 8), half), :]
    send_in.wait_send()
    remote(archive, both_archive.at[1 - y], in_send, in_recv, (partner, c)).wait_recv()
    cross = jnp.concatenate(
        [matern(own_points, both_archive[0] * scaling), matern(own_points, both_archive[1] * scaling)], axis=1)
    columns[y] = cross

    @pl.when(y == 0)
    def _():
        beside_recv(1).wait_recv()

    coupling = split(jnp.transpose(near[1][:, :height]))

    def pass_far(j):
        far_copy(j).wait()
        across_recv(j + 2).wait_recv()
        beside(j + 2).start()

    def turn_far(j):
        beside_recv(j + 2).wait_recv()
        high, low = split(jnp.transpose(far[j].reshape(pair, pair)))
        high_weights[j] = high
        low_weights[j] = low

    for j in range(early):
        @pl.when(z > j)
        def _(j=j):
            pass_far(j)
    for j in range(early):
        @pl.when(z > j)
        def _(j=j):
            turn_far(j)
    across_recv(0).wait_recv()
    upper_inverse = unpack(inverses[0], height)
    lower_inverse = unpack(inverses[1], height)
    upper = split(upper_inverse)
    lower = split(lower_inverse)
    between = split(product(coupling, lower))
    part = half // CHUNKS
    half_count = cands // 2

    def rows_of(k):
        return pl.ds(k * part, part)

    def launch(j, k):
        return remote(columns.at[y, rows_of(k)], panels.at[j, rows_of(k)], out_send.at[0, k], pan_recv.at[j, k],
                      (lax.rem(me + 2, sections), c))

    def to_peer(d, k):
        return remote(columns.at[y, rows_of(k)], peers.at[c, rows_of(k)], out_send.at[1 + d, k], peer_recv.at[c, k],
                      (me, lax.rem(c + 2 * d, cands)))

    def to_sibling(k):
        return remote(columns.at[y, rows_of(k)], peers.at[c, rows_of(k)], out_send.at[1, k], peer_recv.at[c, k],
                      (me, sibling))

    def to_partner(k):
        return remote(columns.at[y, rows_of(k)], columns.at[y, rows_of(k)], out_send.at[1 + half_count, k],
                      out_recv.at[k], (partner, c))

    def emit(j, k):
        if j < steps - 1:
            launch(j, k).start()
        for d in range(1, half_count):
            to_peer(d, k).start()
        to_partner(k).start()
        to_sibling(k).start()

    def solve(k):
        rows = slice(k * part, (k + 1) * part)
        residue = columns[y, rows]
        first = product(split(residue[:, :height]), upper)
        second = product(split(residue[:, height:]), lower) - product(split(first), between)
        columns[y, rows] = jnp.concatenate([first, second], axis=1)

    @pl.when(z == 0)
    def _():
        for k in range(CHUNKS):
            solve(k)
            emit(0, k)

    def onward(j, k):
        return remote(panels.at[j, rows_of(k)], panels.at[j, rows_of(k)], pan_send.at[j, k], pan_recv.at[j, k],
                      (lax.rem(me + 2, sections), c))

    def subtract(j, k, weights):
        onward(j, k).wait_recv()
        if j < steps - 2:
            @pl.when(z < steps - 1)
            def _():
                onward(j, k).start()
        rows = slice(k * part, (k + 1) * part)
        columns[y, rows] = columns[y, rows] - product(split(panels[j, rows]), weights)

    @pl.when(z > 0)
    def _():
        corner = -product(upper, between)
        whole = split(jnp.concatenate([
            jnp.concatenate([upper_inverse, corner], axis=1),
            jnp.concatenate([jnp.zeros((height, height), F32), lower_inverse], axis=1)], axis=0))
        for j in range(steps - 1):
            @pl.when(z > j)
            def _(j=j):
                if j >= early:
                    pass_far(j)
                    turn_far(j)
                high, low = split(product((high_weights[j], low_weights[j]), whole))
                high_weights[j] = high
                low_weights[j] = low
            if j == 0:
                columns[y] = product(split(columns[y]), whole)
        for j in range(steps - 1):
            @pl.when(z > j)
            def _(j=j):
                for k in range(CHUNKS):
                    subtract(j, k, (high_weights[j], low_weights[j]))

                    @pl.when(z == j + 1)
                    def _():
                        emit(j + 1, k)

    def from_peer(q, k):
        return remote(columns.at[y, rows_of(k)], peers.at[q, rows_of(k)], out_send.at[1, k], peer_recv.at[q, k],
                      (me, sibling))

    def pass_on(d, k):
        q = lax.rem(c + 2 * d, cands)
        return remote(peers.at[q, rows_of(k)], peers.at[q, rows_of(k)], pass_send.at[d, k], peer_recv.at[q, k],
                      (me, sibling))

    def wait_peer(q):
        for k in range(CHUNKS):
            from_peer(q, k).wait_recv()

    peers[c] = columns[y]

    @pl.when(c != owner_cand)
    def _():
        remote(candidates, chosen, ch_send.at[0], ch_recv, (me, sibling)).wait_recv()

    points[...] = jnp.transpose(chosen[...] * scaling)
    within = pl.multiple_of((me * slab) % width, 8)
    covariance[...] = matern(points[pl.ds(within, slab), :], own_candidates[...] * scaling)

    for k in range(CHUNKS):
        for d in range(1, half_count):
            from_peer(lax.rem(c + 2 * d, cands), k).wait_recv()
            pass_on(d, k).start()
    for k in range(CHUNKS):
        remote(columns.at[y, rows_of(k)], columns.at[1 - y, rows_of(k)], out_send.at[1, k], out_recv.at[k],
               (partner, c)).wait_recv()
    turned[...] = jnp.transpose(columns[...].reshape(width, pair))
    facing = split(turned[...])

    def piece_copy(q):
        group = 2 * q + y
        return remote(pieces.at[q], sums.at[z, group % ratio], sum_send.at[q],
                      sum_recv.at[z, group % ratio], (group // ratio, c))

    def piece(q):
        group = 2 * q + y
        pieces[q] = product(split(peers[q]), facing)

        @pl.when(group // ratio != me)
        def _():
            piece_copy(q).start()

        @pl.when(group // ratio == me)
        def _():
            sums[z, group % ratio] = pieces[q]

    @pl.when(z < steps - 1)
    def _():
        pl.semaphore_wait(ready, 1)

    @pl.when((z > 0) & (z < steps - 1))
    def _():
        announce()

    piece(c)
    wait_peer(sibling)
    piece(sibling)
    for d in range(1, half_count):
        piece(lax.rem(c + 2 * d, cands))
    for d in range(1, half_count):
        q = lax.rem(sibling + 2 * d, cands)
        wait_peer(q)
        piece(q)

    whitened[...] = turned[pl.ds(pl.multiple_of(y * height, 8), height), :]

    for k in range(ratio):
        for step in range(steps):
            sender = 2 * step + lax.rem(ratio * me + k, 2)

            @pl.when(sender != me)
            def _(k=k, step=step):
                remote(pieces.at[0], sums.at[step, k], sum_send.at[0], sum_recv.at[step, k], (partner, c)).wait_recv()
        total = functools.reduce(jnp.add, [sums[step, k] for step in range(steps)])
        covariance[k * half:(k + 1) * half] = covariance[k * half:(k + 1) * half] - total

    @pl.when(c == owner_cand)
    def _():
        for d in range(1, cands):
            chosen_copy(d).wait_send()
    across(0).wait_send()

    @pl.when(y == 1)
    def _():
        across(1).wait_send()

    @pl.when(y == 0)
    def _():
        beside(1).wait_send()
    for j in range(steps - 1):
        @pl.when(z > j)
        def _(j=j):
            across(j + 2).wait_send()
            beside(j + 2).wait_send()
            if j < steps - 2:
                @pl.when(z < steps - 1)
                def _():
                    for k in range(CHUNKS):
                        onward(j, k).wait_send()

        @pl.when(z == j)
        def _(j=j):
            for k in range(CHUNKS):
                launch(j, k).wait_send()
    for k in range(CHUNKS):
        for d in range(1, half_count):
            to_peer(d, k).wait_send()
            pass_on(d, k).wait_send()
        to_sibling(k).wait_send()
        to_partner(k).wait_send()
    for q in range(cands):
        @pl.when((2 * q + y) // ratio != me)
        def _(q=q):
            piece_copy(q).wait_send()


def shards(sections, cands, archive, candidates, lengths, factor):
    dims, height = archive.shape
    width = candidates.shape[1]
    pair, half, steps = 2 * height, width // 2, sections // 2
    ratio = (2 * cands) // sections
    vmem = pl.BlockSpec(memory_space=pltpu.VMEM)
    hbm = pl.BlockSpec(memory_space=pltpu.HBM)
    dma = pltpu.SemaphoreType.DMA
    return pl.pallas_call(
        functools.partial(kernel, sections, cands),
        out_shape=(jax.ShapeDtypeStruct((height, width), F32), jax.ShapeDtypeStruct((half * ratio, width), F32)),
        in_specs=[hbm] * 4,
        out_specs=(vmem, vmem),
        scratch_shapes=[
            pltpu.VMEM((2, dims, height), F32),
            pltpu.VMEM((2, height, pair), F32),
            pltpu.VMEM((steps - 1, 2, height, pair), F32),
            pltpu.VMEM((dims, width), F32),
            pltpu.VMEM((1, dims), F32),
            pltpu.VMEM((dims, width), F32),
            pltpu.VMEM((width, dims), F32),
            pltpu.VMEM((2, TILE + height // 2, TILE), F32),
            pltpu.VMEM((steps - 1, pair, pair), jnp.bfloat16),
            pltpu.VMEM((steps - 1, pair, pair), jnp.bfloat16),
            pltpu.VMEM((steps - 1, half, pair), F32),
            pltpu.VMEM((cands, half, pair), F32),
            pltpu.VMEM((2, half, pair), F32),
            pltpu.VMEM((pair, width), F32),
            pltpu.VMEM((steps, ratio, half, width), F32),
            pltpu.VMEM((cands, half, width), F32),
            dma((4,)), dma((steps - 1,)),
            dma, dma,
            dma((cands - 1,)), dma,
            dma((steps + 1,)), dma((steps + 1,)), dma((steps + 1,)), dma((steps + 1,)),
            dma((steps - 1, CHUNKS)), dma((steps - 1, CHUNKS)),
            dma((2 + cands // 2, CHUNKS)), dma((CHUNKS,)),
            dma((cands // 2, CHUNKS)), dma((cands, CHUNKS)),
            dma((cands,)), dma((steps, ratio)),
            pltpu.SemaphoreType.REGULAR,
        ],
        compiler_params=pltpu.CompilerParams(
            collective_id=0, has_side_effects=True, vmem_limit_bytes=48 * 1024 * 1024),
    )(*(pltpu.with_memory_space_constraint(x, pltpu.HBM)
        for x in (archive, candidates, lengths.reshape(1, dims), factor)))


def solution(mesh):
    return jax.shard_map(
        functools.partial(shards, mesh.shape["chain"], mesh.shape["cand"]),
        mesh=mesh,
        in_specs=(P(None, "chain"), P(None, "cand"), P(), P("chain", None)),
        out_specs=(P("chain", "cand"), P("chain", "cand")),
        check_vma=False,
    )
```
